256 devices in a mesh: gx: 8 (over y_lo, x), gy: 32 (over z, y_hi, core).
Axes of the slice: x: 4, y: 4 (y_hi: 2, y_lo: 2; y = y_hi * 2 + y_lo), z: 8, core: 2. Of those that a mesh axis runs over, the one named last changes fastest.
Arguments:
- beam_states: bfloat16 [128, 16384], P('gy', 'gx'), may hold values from -6 to 6
- step_tokens: bfloat16 [2, 128, 16384], P(None, 'gy', 'gx'), may hold values from -6 to 6
- norm_gain: bfloat16 [16384], P('gx'), may hold values from 0.25 to 1.75
- w_gate: bfloat16 [16384, 28672], P('gx', 'gy'), may hold values from -0.046875 to 0.046875
- w_up: bfloat16 [16384, 28672], P('gx', 'gy'), may hold values from -0.046875 to 0.046875
- w_down: bfloat16 [28672, 16384], P('gy', 'gx'), may hold values from -0.03125 to 0.03125
- prompt_table: bfloat16 [256, 16384], P(None, 'gx'), may hold values from -6 to 6
- kept_beams: int32 [8], replicated, may hold values from 0 to 127, as said below
- prompt_ids: int32 [8, 16], replicated, may hold values from 0 to 255
Outputs:
- decoded: bfloat16 [128, 16384], P('gy', 'gx')
- evaluated: bfloat16 [128, 16384], P('gy', 'gx')
The draws below stay inside these ranges and needn't reach their ends.
Inputs may be any that keep to these rules, and one draw needn't show every extreme that they name: `kept_beams`: distinct beam indices.
All inputs are finite; a program needn't handle non-finite values.
Results may differ from the reference program's by a relative error of at most 0.014.
Values may be sent and summed in bfloat16 or wider, within the bound.
A program may use at most 64 MiB of HBM per device.

```python
import jax
import jax.numpy as jnp
from jax import lax

D = 16384
FF = 28672
KEPT = 8
PROMPT = 16
PTOK = 256
STEPS = 2
BEAMS = 128


def draw_kept_beams(key, part):
    inner = 1 + jax.random.permutation(jax.random.fold_in(key, 11), BEAMS - 2)[:KEPT - 2]
    ends = jnp.array([0, BEAMS - 1], dtype=jnp.int32)
    whole = jnp.concatenate([ends, inner.astype(jnp.int32)])
    order = jax.random.permutation(jax.random.fold_in(key, 13), KEPT)
    return whole[order].astype(jnp.int32)


def place_ends(values, rng, least, largest):
    place = [jax.random.randint(jax.random.fold_in(rng, axis), (), 0, length) for axis, length in enumerate(values.shape)]
    main_axis = values.shape.index(max(values.shape))
    next_to = place[:main_axis] + [(place[main_axis] + 1) % values.shape[main_axis]] + place[main_axis + 1:]
    return values.at[tuple(place)].set(least).at[tuple(next_to)].set(largest)


def steps_of(stream_key, shape, pieces, low, top_value):
    level = 1.0
    for dim, blocks in pieces:
        steps = jax.random.uniform(jax.random.fold_in(jax.random.fold_in(stream_key, 6), dim), (blocks,), jnp.float32, low / len(pieces), top_value / len(pieces))
        level = level * jnp.repeat(jnp.exp(steps), shape[dim] // blocks).reshape((-1,) + (1,) * (len(shape) - 1 - dim))
    return level


def normal_values(key, shape, spread, bound, cuts=(), kind=jnp.bfloat16):
    result = jax.random.normal(key, shape, jnp.float32) * spread
    if len(cuts) > 0:
        result = steps_of(key, shape, cuts, -0.22, 0.18) * result
    return jnp.clip(result, min=-bound, max=bound).astype(kind)


def setup_inputs(seed: int = 0) -> dict:
    seeds = jax.random.split(jax.random.key(seed), 10)
    beam_states = normal_values(seeds[0], (BEAMS, D), 1.0, 6.0, ((0, 32), (1, 8)))
    step_tokens = normal_values(seeds[1], (STEPS, BEAMS, D), 1.0, 6.0, ((1, 32), (2, 8)))
    norm_gain = jnp.clip(1.0 + 0.15 * jax.random.normal(seeds[2], (D,), jnp.float32), 0.25, 1.75).astype(jnp.bfloat16)
    w_gate = normal_values(seeds[3], (D, FF), D ** -0.5, 0.046875, ((0, 8), (1, 32)))
    w_up = normal_values(seeds[4], (D, FF), D ** -0.5, 0.046875, ((0, 8), (1, 32)))
    w_down = normal_values(seeds[5], (FF, D), FF ** -0.5, 0.03125, ((0, 32), (1, 8)))
    prompt_table = normal_values(seeds[6], (PTOK, D), 1.0, 6.0, ((1, 8),))
    kept_beams = draw_kept_beams(jax.random.fold_in(seeds[9], 71), 0)
    prompt_ids = place_ends(jax.random.randint(seeds[8], (KEPT, PROMPT), 0, PTOK), jax.random.fold_in(seeds[8], 1), 0, PTOK - 1).astype(jnp.int32)
    return {"beam_states": beam_states, "step_tokens": step_tokens, "norm_gain": norm_gain, "w_gate": w_gate, "w_up": w_up, "w_down": w_down, "prompt_table": prompt_table, "kept_beams": kept_beams, "prompt_ids": prompt_ids}


EPS = 1e-05

def layer(rows, norm_gain, w_gate, w_up, w_down):
    values = rows.astype(jnp.float32)
    scale = lax.rsqrt(lax.optimization_barrier(jnp.sum(values * values, axis=1, keepdims=True)) / D + EPS)
    scaled = (values * norm_gain.astype(jnp.float32)).astype(jnp.bfloat16)
    gate = scale * jnp.dot(scaled, w_gate, preferred_element_type=jnp.float32)
    upper = scale * jnp.dot(scaled, w_up, preferred_element_type=jnp.float32)
    hidden = (jax.nn.silu(gate) * upper).astype(jnp.bfloat16)
    return jnp.dot(hidden, w_down, preferred_element_type=jnp.float32)

def reference(beam_states, step_tokens, norm_gain, w_gate, w_up, w_down, prompt_table, kept_beams, prompt_ids):
    state = beam_states
    for step in range(STEPS):
        mixed = (state.astype(jnp.float32) + step_tokens[step].astype(jnp.float32)).astype(jnp.bfloat16)
        state = (mixed.astype(jnp.float32) + layer(mixed, norm_gain, w_gate, w_up, w_down)).astype(jnp.bfloat16)
    chosen = state[kept_beams].astype(jnp.float32)
    words = prompt_table[prompt_ids].astype(jnp.float32)
    rows = (chosen[:, None, :] + words).astype(jnp.bfloat16).reshape(KEPT * PROMPT, D)
    evaluated = (rows.astype(jnp.float32) + layer(rows, norm_gain, w_gate, w_up, w_down)).astype(jnp.bfloat16)
    return (state, evaluated)
```

```python
import functools

import jax
import jax.numpy as jnp
from jax import lax
from jax.experimental import pallas as pl
from jax.experimental.pallas import tpu as pltpu
from jax.sharding import PartitionSpec as P

D = 16384
EPS = 1e-05
BF, F32 = jnp.bfloat16, jnp.float32
NX, NY = 4, 2
NQ = 16
WIDTH = 2048
HID = 896
LAYERS, CHUNKS = 3, 2
MESH = pl.DeviceIdType.MESH

CHIP_STEPS = sorted(range(1, NQ), key=lambda d: -(min(d // 2, 8 - d // 2) + 2 * (d % 2)))
GX_STEPS = sorted(range(1, 8), key=lambda e: -(min(e % 4, 4 - e % 4) + e // 4))


def halves(a, b):
    top = lax.broadcasted_iota(jnp.int32, a.shape, 0) < 4
    return jnp.where(top, a, pltpu.roll(b, 4, 0)), jnp.where(top, pltpu.roll(a, 4, 0), b)


def kernel(
    beam, tok, gain, kept, ids, wg_hbm, wu_hbm, wd_hbm, tab_hbm,
    dec_out, ev_out,
    wg, wu, wd, tab, words, first, x, xs, part, part_in, hid, hid_mm,
    own, sib_out, sib_in, sums, sums_in, tok_out, tok_in,
    pick, pick_sib, pick_all, rows_f, dec_send, dec_in, last, last_in,
    load_sem, snd, first_sem, first_fwd, tok_sem, ag_sem, ag_fwd, rsx_sem, agx_sem,
    sib_sem, rsy_sem, pick_sem, pick_sib_sem, dec_sem, last_sem,
):
    gx, gy = lax.axis_index("gx"), lax.axis_index("gy")
    px, pyl = lax.rem(gx, NX), gx // NX
    core, chip = lax.rem(gy, 2), gy // 2
    yh, z = lax.rem(chip, 2), chip // 2
    other = 1 - core
    sibling = (gx, chip * 2 + other)

    def chip_at(d):
        return lax.rem(z + d // 2, 8) * 2 + lax.rem(yh + d % 2, 2)

    def chip_from(d):
        return lax.rem(z + 8 - d // 2, 8) * 2 + lax.rem(yh + d % 2, 2)

    def gx_at(e):
        return lax.rem(pyl + e // 4, NY) * NX + lax.rem(px + e % 4, NX)

    def gx_from(e):
        return lax.rem(pyl + e // 4, NY) * NX + lax.rem(px + 4 - e % 4, NX)

    def to_chip(q):
        return (gx, q * 2 + core)

    def to_gx(p):
        return (p, gy)

    def remote(src, dst, send, recv, device):
        return pltpu.make_async_remote_copy(
            src_ref=src, dst_ref=dst, send_sem=send, recv_sem=recv, device_id=device, device_id_type=MESH
        )

    sent = []

    loads = [
        pltpu.make_async_copy(s, d, load_sem.at[i])
        for i, (s, d) in enumerate([(tab_hbm, tab), (wg_hbm, wg), (wu_hbm, wu), (wd_hbm, wd)])
    ]
    for load in loads:
        load.start()

    barrier = pltpu.get_barrier_semaphore()
    for d in range(1, NQ):
        pl.semaphore_signal(barrier, inc=1, device_id=to_chip(chip_at(d)), device_id_type=MESH)
    for e in range(1, 8):
        pl.semaphore_signal(barrier, inc=1, device_id=to_gx(gx_at(e)), device_id_type=MESH)
    pl.semaphore_signal(barrier, inc=1, device_id=sibling, device_id_type=MESH)

    mixed = (beam[...].astype(F32) + tok[0].astype(F32)).astype(BF).astype(F32)
    first[core, chip] = jnp.concatenate([mixed[:, :1024], mixed[:, 1024:]], axis=0).astype(BF)
    token = tok[1].astype(F32)
    token = jnp.concatenate([token, token], axis=0).astype(BF)
    for cb in range(NQ):
        tok_out[cb] = token[:, cb * 128 : cb * 128 + 128]

    pl.semaphore_wait(barrier, NQ - 1 + 7 + 1)

    for d in CHIP_STEPS:
        remote(first.at[core, chip], first.at[core, chip], snd.at[0], first_sem.at[d], to_chip(chip_at(d))).start()
    remote(first.at[core, chip], first.at[core, chip], snd.at[1], first_fwd.at[0], sibling).start()
    for d in CHIP_STEPS:
        remote(tok_out.at[chip_at(d)], tok_in.at[chip], snd.at[2], tok_sem.at[d], to_chip(chip_at(d))).start()
    sent.append((first.at[0, pl.ds(0, NQ - 1)], snd.at[0]))
    sent.append((first.at[0], snd.at[1]))
    sent.append((tok_in.at[pl.ds(0, NQ - 1)], snd.at[2]))
    tok_in[chip] = tok_out[chip]

    loads[0].wait()
    lookup = (ids[...] == lax.broadcasted_iota(jnp.int32, (128, 256), 1)).astype(F32).astype(BF)
    for n in range(4):
        cols = slice(n * 512, n * 512 + 512)
        words[:, cols] = jnp.dot(lookup, tab[:, cols], preferred_element_type=F32).astype(BF)

    for d in reversed(CHIP_STEPS):
        q = chip_from(d)
        piece = first.at[core, q]
        remote(piece, piece, snd.at[0], first_sem.at[d], to_chip(chip_at(d))).wait_recv()
        remote(piece, piece, snd.at[1], first_fwd.at[0], sibling).start()
    remote(first.at[other], first.at[other], snd.at[1], first_fwd.at[0], sibling).wait_recv()
    for load in loads[1:3]:
        load.wait()

    def prepare(layer, k):
        squares = []
        for h in range(2):
            total = jnp.zeros((32, 128), F32)
            for cb in range(NQ):
                v = x[layer, k, h, cb].astype(F32)
                total = total + v * v
                cols = slice(cb * 128, cb * 128 + 128)
                xs[h * 32 : h * 32 + 32, cols] = (v * gain[:, cols].astype(F32)).astype(BF)
            squares.append(jnp.sum(total, axis=1, keepdims=True))
        whole = jnp.broadcast_to(jnp.concatenate(squares, axis=0), (64, 128))
        high = whole.astype(BF).astype(F32)
        both = jnp.concatenate([high.reshape(8, 8, 128), (whole - high).reshape(8, 8, 128)], axis=1)
        part[layer, k, :, :, HID:1024] = both.astype(BF)

    def up(layer, k):
        rows = xs[...]

        def tile(n, carry):
            cols = pl.ds(pl.multiple_of(n * 128, 128), 128)
            weights = jnp.concatenate([wg[:, cols], wu[:, cols]], axis=1)
            y = jnp.dot(rows, weights, preferred_element_type=F32)
            both = jnp.concatenate([y[:, :128].reshape(8, 8, 128), y[:, 128:].reshape(8, 8, 128)], axis=1)
            part[layer, k, :, :, cols] = both.astype(BF)
            return carry

        lax.fori_loop(0, HID // 128, tile, 0)
        i = layer * CHUNKS + k
        for e in GX_STEPS:
            p = gx_at(e)
            remote(part.at[layer, k, p], part_in.at[layer, k, e], snd.at[10 + i], rsx_sem.at[i], to_gx(p)).start()
        sent.append((part_in.at[layer, k, pl.ds(1, 7)], snd.at[10 + i]))

    def act(layer, k):
        i = layer * CHUNKS + k
        arrived = part_in.at[layer, k, pl.ds(1, 7)]
        remote(arrived, arrived, snd.at[10 + i], rsx_sem.at[i], to_gx(gx)).wait_recv()
        total = part[layer, k, gx].astype(F32)
        for e in range(1, 8):
            total = total + part_in[layer, k, e].astype(F32)
        squares = total[0:8, HID:1024] + total[8:16, HID:1024]
        scale = lax.rsqrt(squares / D + EPS)
        for n in range(HID // 128):
            cols = slice(n * 128, n * 128 + 128)
            g = scale * total[0:8, cols]
            u = scale * total[8:16, cols]
            hid[layer, k, gx, :, cols] = (g / (1.0 + jnp.exp(-g)) * u).astype(BF)
        piece = hid.at[layer, k, gx]
        for e in GX_STEPS:
            remote(piece, piece, snd.at[20 + i], agx_sem.at[i, e], to_gx(gx_at(e))).start()
        sent.append((hid.at[layer, k, pl.ds(0, 7)], snd.at[20 + i]))

    def down(layer, k):
        i = layer * CHUNKS + k
        for e in reversed(GX_STEPS):
            piece = hid.at[layer, k, gx_from(e)]
            remote(piece, piece, snd.at[20 + i], agx_sem.at[i, e], to_gx(gx)).wait_recv()
        hid_mm[...] = hid[layer, k].astype(F32).reshape(64, HID).astype(BF)
        rows = hid_mm[...]

        def tile(n, carry):
            cols = pl.ds(pl.multiple_of(n * 256, 128), 256)
            y = jnp.dot(rows, wd[:, cols], preferred_element_type=F32)
            mine = jnp.where(core == 0, y[0:32], y[32:64])
            theirs = jnp.where(core == 0, y[32:64], y[0:32]).astype(BF)
            for m in range(2):
                own[k, 2 * n + m] = mine[:, m * 128 : m * 128 + 128]
                sib_out[layer, k, 2 * n + m] = theirs[:, m * 128 : m * 128 + 128]
            return carry

        lax.fori_loop(0, 8, tile, 0)
        remote(sib_out.at[layer, k], sib_in.at[layer, k], snd.at[30 + i], sib_sem.at[i], sibling).start()
        sent.append((sib_out.at[layer, k], snd.at[30 + i]))

    def scatter(layer, k):
        i = layer * CHUNKS + k
        remote(sib_in.at[layer, k], sib_in.at[layer, k], snd.at[30 + i], sib_sem.at[i], sibling).wait_recv()
        for cb in range(NQ):
            sums[layer, k, cb] = (own[k, cb] + sib_in[layer, k, cb].astype(F32)).astype(BF)
        for d in CHIP_STEPS:
            q = chip_at(d)
            remote(sums.at[layer, k, q], sums_in.at[layer, k, d], snd.at[40 + i], rsy_sem.at[i], to_chip(q)).start()
        sent.append((sums_in.at[layer, k, pl.ds(1, NQ - 1)], snd.at[40 + i]))

    def new_state(layer, k):
        i = layer * CHUNKS + k
        arrived = sums_in.at[layer, k, pl.ds(1, NQ - 1)]
        remote(arrived, arrived, snd.at[40 + i], rsy_sem.at[i], sibling).wait_recv()
        total = sums[layer, k, chip].astype(F32)
        for d in range(1, NQ):
            total = total + sums_in[layer, k, d].astype(F32)
        return (x[layer, k, core, chip].astype(F32) + total).astype(BF).astype(F32)

    def spread(k):
        state = new_state(0, k)
        if k == 0:
            for d in CHIP_STEPS:
                piece = tok_in.at[chip_from(d)]
                remote(piece, piece, snd.at[2], tok_sem.at[d], sibling).wait_recv()
        groups = []
        for g in range(4):
            a, b = tok_in[8 * k + 2 * g].astype(F32), tok_in[8 * k + 2 * g + 1].astype(F32)
            groups.append(jnp.where(lax.broadcasted_iota(jnp.int32, (8, 128), 0) < 4, a, b))
        x[1, k, core, chip] = (state + jnp.concatenate(groups, axis=0)).astype(BF)
        piece = x.at[1, k, core, chip]
        for d in CHIP_STEPS:
            remote(piece, piece, snd.at[3 + k], ag_sem.at[k, d], to_chip(chip_at(d))).start()
        remote(piece, piece, snd.at[5 + k], ag_fwd.at[k], sibling).start()
        sent.append((x.at[1, k, 0, pl.ds(0, NQ - 1)], snd.at[3 + k]))
        sent.append((x.at[1, k, 0], snd.at[5 + k]))

    def collect(k):
        for d in reversed(CHIP_STEPS):
            piece = x.at[1, k, core, chip_from(d)]
            remote(piece, piece, snd.at[3 + k], ag_sem.at[k, d], sibling).wait_recv()
            remote(piece, piece, snd.at[5 + k], ag_fwd.at[k], sibling).start()
        theirs = x.at[1, k, other]
        remote(theirs, theirs, snd.at[5 + k], ag_fwd.at[k], sibling).wait_recv()

    for k in range(CHUNKS):
        for h in range(2):
            for g in range(4):
                a, b = first[h, 8 * k + 2 * g].astype(F32), first[h, 8 * k + 2 * g + 1].astype(F32)
                low, high = halves(a, b)
                rows_f[h, 4 * k + g, :, 0:1024] = low
                rows_f[h, 4 * k + g, :, 1024:2048] = high
            for cb in range(NQ):
                block = rows_f[h, 4 * k : 4 * k + 4, :, cb * 128 : cb * 128 + 128]
                x[0, k, h, cb] = block.reshape(32, 128).astype(BF)
        prepare(0, k)
        up(0, k)
    for k in range(CHUNKS):
        act(0, k)
    loads[3].wait()
    for k in range(CHUNKS):
        down(0, k)
    for k in range(CHUNKS):
        scatter(0, k)
    for k in range(CHUNKS):
        spread(k)

    for k in range(CHUNKS):
        collect(k)
        prepare(1, k)
        up(1, k)
    for k in range(CHUNKS):
        act(1, k)
    for k in range(CHUNKS):
        down(1, k)
    for k in range(CHUNKS):
        scatter(1, k)

    chosen = jnp.zeros((8, 128), F32)
    for k in range(CHUNKS):
        state = new_state(1, k)
        t = lax.broadcasted_iota(jnp.int32, (8, 32), 1)
        beam_of = (8 * k + t // 4) * 8 + 4 * core + lax.rem(t, 4)
        picker = (kept[...] == beam_of).astype(F32).astype(BF)
        chosen = chosen + jnp.dot(picker, state.astype(BF), preferred_element_type=F32)
        dec_send[k] = state.reshape(4, 8, 128).astype(BF)
    pick[...] = chosen
    remote(pick, pick_sib, snd.at[7], pick_sib_sem.at[0], sibling).start()
    remote(pick, pick_sib, snd.at[7], pick_sib_sem.at[0], sibling).wait_recv()
    pick_all[chip] = chosen + pick_sib[...]
    piece = pick_all.at[chip]
    for d in CHIP_STEPS:
        remote(piece, piece, snd.at[8], pick_sem.at[d], to_chip(chip_at(d))).start()
    sent.append((pick, snd.at[7]))
    sent.append((pick_all.at[pl.ds(0, NQ - 1)], snd.at[8]))

    def rel(src, dst):
        return lax.rem(src - dst + NQ, NQ)

    for k in range(CHUNKS):
        for g in range(4):
            for b in range(2):
                q = 8 * k + 2 * g + b

                @pl.when(q != chip)
                def _():
                    remote(dec_send.at[k, g], dec_in.at[rel(chip, q)], snd.at[9], dec_sem.at[0], to_chip(q)).start()

                @pl.when(q == chip)
                def _():
                    dec_in[0] = dec_send[k, g]

    sent.append((dec_in.at[pl.ds(1, NQ - 1)], snd.at[9]))
    for d in reversed(CHIP_STEPS):
        arrived = pick_all.at[chip_from(d)]
        remote(arrived, arrived, snd.at[8], pick_sem.at[d], sibling).wait_recv()

    for k in range(CHUNKS):
        for h in range(2):
            for cb in range(NQ):
                cols = slice(cb * 128, cb * 128 + 128)
                w = words[h * 64 + 32 * k : h * 64 + 32 * k + 32, cols].astype(F32)
                c = jnp.concatenate(
                    [jnp.broadcast_to(pick_all[cb, 4 * k + g : 4 * k + g + 1], (8, 128)) for g in range(4)], axis=0
                )
                rows = (c + w).astype(BF)
                x[2, k, h, cb] = rows
                rows_f[h, 4 * k : 4 * k + 4, :, cols] = rows.astype(F32).reshape(4, 8, 128)
        prepare(2, k)
        up(2, k)

    arrived = dec_in.at[pl.ds(1, NQ - 1)]
    remote(arrived, arrived, snd.at[9], dec_sem.at[0], sibling).wait_recv()
    for cb in range(NQ):
        both = dec_in[rel(cb, chip)].astype(F32)
        dec_out[:, cb * 128 : cb * 128 + 128] = jnp.where(yh == 0, both[0:4], both[4:8]).astype(BF)

    for k in range(CHUNKS):
        act(2, k)
    for k in range(CHUNKS):
        down(2, k)
    for k in range(CHUNKS):
        i = 2 * CHUNKS + k
        remote(sib_in.at[2, k], sib_in.at[2, k], snd.at[30 + i], sib_sem.at[i], sibling).wait_recv()
        for n in range(8):
            left = own[k, n] + sib_in[2, k, n].astype(F32)
            right = own[k, n + 8] + sib_in[2, k, n + 8].astype(F32)
            for g in range(4):
                even, odd = halves(left[8 * g : 8 * g + 8], right[8 * g : 8 * g + 8])
                last[8 * k + 2 * g, :, n * 128 : n * 128 + 128] = even.astype(BF)
                last[8 * k + 2 * g + 1, :, n * 128 : n * 128 + 128] = odd.astype(BF)
        for g in range(4):
            for b in range(2):
                q = 8 * k + 2 * g + b

                @pl.when(q != chip)
                def _():
                    remote(last.at[q], last_in.at[rel(chip, q)], snd.at[40 + i], last_sem.at[0], to_chip(q)).start()

    @pl.when(chip < 8)
    def _():
        remote(last.at[pl.ds(0, 7)], last.at[pl.ds(0, 7)], snd.at[44], last_sem.at[0], sibling).wait_send()
        remote(last.at[pl.ds(8, 8)], last.at[pl.ds(8, 8)], snd.at[45], last_sem.at[0], sibling).wait_send()

    @pl.when(chip >= 8)
    def _():
        remote(last.at[pl.ds(0, 8)], last.at[pl.ds(0, 8)], snd.at[44], last_sem.at[0], sibling).wait_send()
        remote(last.at[pl.ds(8, 7)], last.at[pl.ds(8, 7)], snd.at[45], last_sem.at[0], sibling).wait_send()

    for ref, sem in sent:
        remote(ref, ref, sem, sem, sibling).wait_send()

    arrived = last_in.at[pl.ds(1, NQ - 1)]
    remote(arrived, arrived, snd.at[44], last_sem.at[0], sibling).wait_recv()
    total = last[chip].astype(F32)
    for s in range(1, NQ):
        total = total + last_in[s].astype(F32)
    mine = rows_f[core, z]
    even, odd = halves(mine[:, 0:1024], mine[:, 1024:2048])
    result = (jnp.where(yh == 0, even, odd) + total).astype(BF).astype(F32)
    ev_out[:, 0:1024] = result[0:4].astype(BF)
    ev_out[:, 1024:2048] = result[4:8].astype(BF)


def on_device(
    beam_states, step_tokens, norm_gain, w_gate, w_up, w_down, prompt_table, kept_beams, prompt_ids
):
    ids = prompt_ids.reshape(16, 2, 4).transpose(1, 0, 2).reshape(128, 1)
    vmem = pl.BlockSpec(memory_space=pltpu.VMEM)
    hbm = pl.BlockSpec(memory_space=pl.ANY)
    V, dma = pltpu.VMEM, pltpu.SemaphoreType.DMA
    n = LAYERS * CHUNKS
    scratch = [
        V((WIDTH, HID), BF), V((WIDTH, HID), BF), V((HID, WIDTH), BF), V((256, WIDTH), BF),
        V((128, WIDTH), BF),
        V((2, NQ, 8, 1024), BF),
        V((LAYERS, CHUNKS, 2, NQ, 32, 128), BF),
        V((64, WIDTH), BF),
        V((LAYERS, CHUNKS, 8, 16, 1024), BF), V((LAYERS, CHUNKS, 8, 16, 1024), BF),
        V((LAYERS, CHUNKS, 8, 8, HID), BF), V((64, HID), BF),
        V((CHUNKS, NQ, 32, 128), F32),
        V((LAYERS, CHUNKS, NQ, 32, 128), BF), V((LAYERS, CHUNKS, NQ, 32, 128), BF),
        V((2, CHUNKS, NQ, 32, 128), BF), V((2, CHUNKS, NQ, 32, 128), BF),
        V((NQ, 8, 128), BF), V((NQ, 8, 128), BF),
        V((8, 128), F32), V((8, 128), F32), V((NQ, 8, 128), F32),
        V((2, 8, 8, WIDTH), F32),
        V((CHUNKS, 4, 8, 128), BF), V((NQ, 8, 128), BF),
        V((NQ, 8, 1024), BF), V((NQ, 8, 1024), BF),
        dma((4,)), dma((50,)), dma((NQ,)), dma((1,)), dma((NQ,)),
        dma((CHUNKS, NQ)), dma((CHUNKS,)), dma((n,)), dma((n, 8)),
        dma((n,)), dma((n,)), dma((NQ,)), dma((1,)), dma((1,)), dma((1,)),
    ]
    return pl.pallas_call(
        kernel,
        out_shape=(jax.ShapeDtypeStruct((4, WIDTH), BF), jax.ShapeDtypeStruct((4, WIDTH), BF)),
        in_specs=[vmem] * 5 + [hbm] * 4,
        out_specs=(vmem, vmem),
        scratch_shapes=scratch,
        compiler_params=pltpu.CompilerParams(
            collective_id=0, has_side_effects=True, vmem_limit_bytes=48 * 2**20
        ),
        name="beam_steps",
    )(
        beam_states, step_tokens, norm_gain.reshape(1, WIDTH), kept_beams.reshape(8, 1), ids,
        w_gate, w_up, w_down, prompt_table,
    )


def solution(mesh):
    return jax.shard_map(
        on_device,
        mesh=mesh,
        in_specs=(
            P("gy", "gx"),
            P(None, "gy", "gx"),
            P("gx"),
            P("gx", "gy"),
            P("gx", "gy"),
            P("gy", "gx"),
            P(None, "gx"),
            P(),
            P(),
        ),
        out_specs=(P("gy", "gx"), P("gy", "gx")),
        check_vma=False,
    )
```

```python
import jax
import jax.numpy as jnp
from jax import lax
from jax.experimental import pallas as pl
from jax.experimental.pallas import tpu as pltpu
from jax.sharding import PartitionSpec as P

D = 16384
EPS = 1e-05
BF, F32 = jnp.bfloat16, jnp.float32
NX, NY = 4, 2
NQ = 16
WIDTH = 2048
HID = 896
LAYERS, CHUNKS = 3, 2
MESH = pl.DeviceIdType.MESH

CHIP_STEPS = sorted(range(1, NQ), key=lambda d: -(min(d // 2, 8 - d // 2) + 2 * (d % 2)))
GX_STEPS = sorted(range(1, 8), key=lambda e: -(min(e % 4, 4 - e % 4) + e // 4))


def swap(a, b, rows):
    first = lax.rem(lax.broadcasted_iota(jnp.int32, a.shape, 0), 2 * rows) < rows
    return jnp.where(first, a, pltpu.roll(b, rows, 0)), jnp.where(first, pltpu.roll(a, 8 - rows, 0), b)


def turn(a):
    a0, a2 = swap(a[0], a[2], 4)
    a1, a3 = swap(a[1], a[3], 4)
    return (*swap(a0, a1, 2), *swap(a2, a3, 2))


def kernel(
    beam_hbm, tok_hbm, gain_hbm, kept_hbm, ids_hbm, wg_hbm, wu_hbm, wd_hbm, tab_hbm,
    dec_out, ev_out,
    beam, tok, gain, kept, ids, wg, wu, wd, tab, words, first, x, xs, part, part_in, hid, hid_mm,
    own, sib_out, sib_in, sums, sums_in, tok_out, tok_in,
    kp, kp_out, kp_in, ks, ks_in, pick_all, rows_f, dec_send, dec_in, last, last_in,
    load_sem, snd, first_sem, first_fwd, tok_sem, ag_sem, ag_fwd, rsx_sem, agx_sem,
    sib_sem, rsy_sem, kp_sem, ks_sem, pick_sem, dec_sem, last_sem,
):
    gx, gy = lax.axis_index("gx"), lax.axis_index("gy")
    px, pyl = lax.rem(gx, NX), gx // NX
    core, chip = lax.rem(gy, 2), gy // 2
    yh, z = lax.rem(chip, 2), chip // 2
    other = 1 - core
    sibling = (gx, chip * 2 + other)

    def chip_at(d):
        return lax.rem(z + d // 2, 8) * 2 + lax.rem(yh + d % 2, 2)

    def chip_from(d):
        return lax.rem(z + 8 - d // 2, 8) * 2 + lax.rem(yh + d % 2, 2)

    def gx_at(e):
        return lax.rem(pyl + e // 4, NY) * NX + lax.rem(px + e % 4, NX)

    def gx_from(e):
        return lax.rem(pyl + e // 4, NY) * NX + lax.rem(px + 4 - e % 4, NX)

    def to_chip(q):
        return (gx, q * 2 + core)

    def to_gx(p):
        return (p, gy)

    def remote(src, dst, send, recv, device):
        return pltpu.make_async_remote_copy(
            src_ref=src, dst_ref=dst, send_sem=send, recv_sem=recv, device_id=device, device_id_type=MESH
        )

    def arrived(ref, recv):
        remote(ref, ref, snd.at[0], recv, sibling).wait_recv()

    sent = []

    def sending(ref):
        sent.append(ref)
        return snd.at[len(sent) - 1]

    pairs = [
        (beam_hbm, beam), (tok_hbm, tok), (tab_hbm, tab), (ids_hbm, ids), (kept_hbm, kept), (gain_hbm, gain),
        (wg_hbm, wg), (wu_hbm, wu), (wd_hbm, wd),
    ]
    loads = [pltpu.make_async_copy(s, d, load_sem.at[i]) for i, (s, d) in enumerate(pairs)]
    for load in loads:
        load.start()

    barrier = pltpu.get_barrier_semaphore()
    for d in CHIP_STEPS:
        pl.semaphore_signal(barrier, inc=1, device_id=to_chip(chip_at(d)), device_id_type=MESH)
    for e in GX_STEPS:
        pl.semaphore_signal(barrier, inc=1, device_id=to_gx(gx_at(e)), device_id_type=MESH)
    pl.semaphore_signal(barrier, inc=1, device_id=sibling, device_id_type=MESH)

    loads[0].wait()
    loads[1].wait()
    mixed = (beam[...].astype(F32) + tok[0].astype(F32)).astype(BF).astype(F32)
    mixed = jnp.concatenate([mixed, mixed], axis=0)
    top = lax.broadcasted_iota(jnp.int32, (8, 512), 0) < 4
    even, odd = swap(
        jnp.where(top, mixed[:, 0:512], mixed[:, 1024:1536]), jnp.where(top, mixed[:, 512:1024], mixed[:, 1536:2048]), 2
    )
    first[0, core, chip] = even.astype(BF)
    first[1, core, chip] = odd.astype(BF)
    token = tok[1].astype(F32)
    token = jnp.concatenate([token, token], axis=0).astype(BF)
    for cb in range(NQ):
        tok_out[cb] = token[:, cb * 128 : cb * 128 + 128]

    pl.semaphore_wait(barrier, NQ - 1 + 7 + 1)

    forward = []
    for k in range(CHUNKS):
        piece = first.at[k, core, chip]
        sem = sending(first.at[k, 0, pl.ds(0, NQ - 1)])
        forward.append(sending(first.at[k, 0]))
        for d in CHIP_STEPS:
            remote(piece, piece, sem, first_sem.at[k, d], to_chip(chip_at(d))).start()
        remote(piece, piece, forward[k], first_fwd.at[k], sibling).start()
    sem = sending(tok_in.at[pl.ds(0, NQ - 1)])
    for d in CHIP_STEPS:
        remote(tok_out.at[chip_at(d)], tok_in.at[chip], sem, tok_sem.at[d], to_chip(chip_at(d))).start()
    tok_in[chip] = tok_out[chip]

    for load in loads[2:6]:
        load.wait()

    def row_of(shape, dim):
        t = lax.broadcasted_iota(jnp.int32, shape, dim)
        return 8 * (lax.rem(t, 32) // 2) + 4 * (lax.rem(t, 64) // 32) + 2 * (t // 64) + lax.rem(t, 2)

    of_beam = (row_of((128, 8), 0) // 16 == lax.broadcasted_iota(jnp.int32, (128, 8), 1)).astype(F32).astype(BF)
    beam_ids = jnp.dot(of_beam, ids[...].astype(F32).astype(BF), preferred_element_type=F32)
    place = lax.rem(row_of((128, 16), 0), 16) == lax.broadcasted_iota(jnp.int32, (128, 16), 1)
    row_ids = jnp.sum(jnp.where(place, beam_ids, 0.0), axis=1, keepdims=True)
    lookup = (row_ids == lax.broadcasted_iota(jnp.int32, (128, 256), 1).astype(F32)).astype(F32).astype(BF)
    for n in range(4):
        cols = slice(n * 512, n * 512 + 512)
        words[:, cols] = jnp.dot(lookup, tab[:, cols], preferred_element_type=F32).astype(BF)
    nth = lax.broadcasted_iota(jnp.int32, (16, 128), 0)
    kept_rows = jnp.full((16, 128), -1, jnp.int32)
    for n in range(8):
        kept_rows = jnp.where(nth == n, kept[n], kept_rows)
    picker = (kept_rows == row_of((16, 128), 1)).astype(F32).astype(BF)

    def prepare(layer, k):
        squares = []
        for h in range(2):
            total = jnp.zeros((32, 128), F32)
            for cb in range(NQ):
                v = x[layer, k, h, cb].astype(F32)
                total = total + v * v
                cols = slice(cb * 128, cb * 128 + 128)
                xs[h * 32 : h * 32 + 32, cols] = (v * gain[cols].astype(F32)[None, :]).astype(BF)
            squares.append(jnp.sum(total, axis=1, keepdims=True))
        whole = jnp.broadcast_to(jnp.concatenate(squares, axis=0), (64, 128))
        high = whole.astype(BF).astype(F32)
        both = jnp.concatenate([high.reshape(8, 8, 128), (whole - high).reshape(8, 8, 128)], axis=1)
        part[layer, k, :, :, HID:1024] = both.astype(BF)

    def up(layer, k):
        rows = xs[...]

        def tile(n, carry):
            cols = pl.ds(pl.multiple_of(n * 128, 128), 128)
            weights = jnp.concatenate([wg[:, cols], wu[:, cols]], axis=1)
            y = jnp.dot(rows, weights, preferred_element_type=F32)
            both = jnp.concatenate([y[:, :128].reshape(8, 8, 128), y[:, 128:].reshape(8, 8, 128)], axis=1)
            part[layer, k, :, :, cols] = both.astype(BF)
            return carry

        lax.fori_loop(0, HID // 128, tile, 0)
        sem = sending(part_in.at[layer, k, pl.ds(1, 7)])
        for e in GX_STEPS:
            p = gx_at(e)
            remote(part.at[layer, k, p], part_in.at[layer, k, e], sem, rsx_sem.at[layer, k], to_gx(p)).start()

    def act(layer, k):
        arrived(part_in.at[layer, k, pl.ds(1, 7)], rsx_sem.at[layer, k])
        total = part[layer, k, gx].astype(F32)
        for e in range(1, 8):
            total = total + part_in[layer, k, e].astype(F32)
        squares = total[0:8, HID:1024] + total[8:16, HID:1024]
        scale = lax.rsqrt(squares / D + EPS)
        for n in range(HID // 128):
            cols = slice(n * 128, n * 128 + 128)
            g = scale * total[0:8, cols]
            u = scale * total[8:16, cols]
            hid[layer, k, gx, :, cols] = (g / (1.0 + jnp.exp(-g)) * u).astype(BF)
        piece = hid.at[layer, k, gx]
        sem = sending(hid.at[layer, k, pl.ds(0, 7)])
        for e in GX_STEPS:
            remote(piece, piece, sem, agx_sem.at[layer, k, e], to_gx(gx_at(e))).start()

    def hidden(layer, k):
        for e in reversed(GX_STEPS):
            arrived(hid.at[layer, k, gx_from(e)], agx_sem.at[layer, k, e])
        hid_mm[k, 0:64] = hid[layer, k].astype(F32).reshape(64, HID).astype(BF)

    def down(layer, k, with_kept=False):
        rows = hid_mm[k] if with_kept else hid_mm[k, 0:64]

        def tile(n, carry):
            cols = pl.ds(pl.multiple_of(n * 256, 128), 256)
            y = jnp.dot(rows, wd[:, cols], preferred_element_type=F32)
            mine = jnp.where(core == 0, y[0:32], y[32:64])
            theirs = jnp.where(core == 0, y[32:64], y[0:32]).astype(BF)
            for m in range(2):
                own[layer, k, 2 * n + m] = mine[:, m * 128 : m * 128 + 128]
                sib_out[layer, k, 2 * n + m] = theirs[:, m * 128 : m * 128 + 128]
                if with_kept:
                    kp[2 * n + m] = y[64:72, m * 128 : m * 128 + 128]
            return carry

        lax.fori_loop(0, 8, tile, 0)
        if with_kept:
            kp_out[...] = kp[pl.ds(8 * other, 8)].astype(BF)
            remote(kp_out, kp_in, sending(kp_out), kp_sem.at[0], sibling).start()
        sem = sending(sib_out.at[layer, k])
        remote(sib_out.at[layer, k], sib_in.at[layer, k], sem, sib_sem.at[layer, k], sibling).start()

    def scatter(layer, k):
        arrived(sib_in.at[layer, k], sib_sem.at[layer, k])
        sem = sending(sums_in.at[layer, k, pl.ds(1, NQ - 1)])
        for d in CHIP_STEPS:
            q = chip_at(d)
            sums[layer, k, q] = (own[layer, k, q] + sib_in[layer, k, q].astype(F32)).astype(BF)
            remote(sums.at[layer, k, q], sums_in.at[layer, k, d], sem, rsy_sem.at[layer, k], to_chip(q)).start()

    def new_state(layer, k):
        arrived(sums_in.at[layer, k, pl.ds(1, NQ - 1)], rsy_sem.at[layer, k])
        total = own[layer, k, chip] + sib_in[layer, k, chip].astype(F32)
        for d in range(1, NQ):
            total = total + sums_in[layer, k, d].astype(F32)
        return (x[layer, k, core, chip].astype(F32) + total).astype(BF).astype(F32)

    second_fwd = []

    def spread(k):
        state = new_state(0, k)
        if k == 0:
            for d in CHIP_STEPS:
                arrived(tok_in.at[chip_from(d)], tok_sem.at[d])
        pair = lax.broadcasted_iota(jnp.int32, (8, 128), 0) // 2
        groups = []
        for g in range(4):
            group = jnp.zeros((8, 128), F32)
            for a in range(4):
                t = tok_in[4 * g + a].astype(F32)
                group = jnp.where(pair == a, t if a % 2 == k else pltpu.roll(t, 2, 0), group)
            groups.append(group)
        x[1, k, core, chip] = (state + jnp.concatenate(groups, axis=0)).astype(BF)
        piece = x.at[1, k, core, chip]
        sem = sending(x.at[1, k, 0, pl.ds(0, NQ - 1)])
        second_fwd.append(sending(x.at[1, k, 0]))
        for d in CHIP_STEPS:
            remote(piece, piece, sem, ag_sem.at[k, d], to_chip(chip_at(d))).start()
        remote(piece, piece, second_fwd[k], ag_fwd.at[k], sibling).start()

    def collect(k):
        for d in reversed(CHIP_STEPS):
            piece = x.at[1, k, core, chip_from(d)]
            arrived(piece, ag_sem.at[k, d])
            remote(piece, piece, second_fwd[k], ag_fwd.at[k], sibling).start()
        arrived(x.at[1, k, other], ag_fwd.at[k])

    for k in range(CHUNKS):
        for d in reversed(CHIP_STEPS):
            piece = first.at[k, core, chip_from(d)]
            arrived(piece, first_sem.at[k, d])
            remote(piece, piece, forward[k], first_fwd.at[k], sibling).start()
        arrived(first.at[k, other], first_fwd.at[k])
        for h in range(2):
            for g in range(4):
                quarters = turn([first[k, h, 4 * g + a].astype(F32) for a in range(4)])
                for m in range(4):
                    rows_f[k, h, g, :, m * 512 : m * 512 + 512] = quarters[m]
            for cb in range(NQ):
                block = rows_f[k, h, :, :, cb * 128 : cb * 128 + 128]
                x[0, k, h, cb] = block.reshape(32, 128).astype(BF)
        prepare(0, k)
        if k == 0:
            loads[6].wait()
            loads[7].wait()
        up(0, k)
    for k in range(CHUNKS):
        act(0, k)
    loads[8].wait()
    for k in range(CHUNKS):
        hidden(0, k)
        down(0, k)
    for k in range(CHUNKS):
        scatter(0, k)
    for k in range(CHUNKS):
        spread(k)

    for k in range(CHUNKS):
        collect(k)
        prepare(1, k)
        up(1, k)
    for k in range(CHUNKS):
        act(1, k)
    kept_mixed = []
    for m in range(8):
        cb = 8 * core + m
        column = jnp.concatenate([x[1, k, h, cb] for k in range(CHUNKS) for h in range(2)], axis=0)
        kept_mixed.append(jnp.dot(picker, column, preferred_element_type=F32)[0:8])
    for k in range(CHUNKS):
        hidden(1, k)

    def pick_hidden(n, carry):
        cols = pl.ds(pl.multiple_of(n * 128, 128), 128)
        chosen = jnp.zeros((16, 128), F32)
        for k in range(CHUNKS):
            rows = picker[:, 64 * k : 64 * k + 64]
            chosen = chosen + jnp.dot(rows, hid_mm[k, 0:64, cols], preferred_element_type=F32)
        hid_mm[1, 64:80, cols] = chosen.astype(BF)
        return carry

    lax.fori_loop(0, HID // 128, pick_hidden, 0)
    down(1, 1, True)
    down(1, 0)

    arrived(kp_in, kp_sem.at[0])
    ks[...] = (kp[pl.ds(8 * core, 8)] + kp_in[...].astype(F32)).astype(BF)
    sem = sending(ks_in.at[pl.ds(1, NQ - 1)])
    for d in CHIP_STEPS:
        remote(ks, ks_in.at[d], sem, ks_sem.at[0], to_chip(chip_at(d))).start()
    arrived(ks_in.at[pl.ds(1, NQ - 1)], ks_sem.at[0])
    total = ks[...].astype(F32)
    for d in range(1, NQ):
        total = total + ks_in[d].astype(F32)
    for m in range(8):
        pick_all[8 * core + m] = (kept_mixed[m] + total[m]).astype(BF)
    half = pick_all.at[pl.ds(8 * core, 8)]
    remote(half, half, sending(half), pick_sem.at[0], sibling).start()
    arrived(half, pick_sem.at[0])

    upper = lax.broadcasted_iota(jnp.int32, (8, 128), 0) < 4
    for k in range(CHUNKS):
        for cb in range(NQ):
            cols = slice(cb * 128, cb * 128 + 128)
            chosen = pick_all[cb].astype(F32)
            chosen = jnp.concatenate(
                [jnp.where(upper, chosen[2 * g : 2 * g + 1], chosen[2 * g + 1 : 2 * g + 2]) for g in range(4)], axis=0
            )
            for h in range(2):
                at = 64 * k + 32 * h
                rows = (chosen + words[at : at + 32, cols].astype(F32)).astype(BF)
                x[2, k, h, cb] = rows
                rows_f[k, h, :, :, cols] = rows.astype(F32).reshape(4, 8, 128)
        prepare(2, k)
        up(2, k)

    for k in range(CHUNKS):
        scatter(1, k)
    for k in range(CHUNKS):
        act(2, k)
    for k in range(CHUNKS):
        state = new_state(1, k).reshape(4, 8, 128)
        dec_send[:, 8 * k : 8 * k + 8, :] = state.astype(BF)
    sem = sending(dec_in.at[pl.ds(1, NQ - 1)])
    for d in CHIP_STEPS:
        q = chip_at(d)
        remote(dec_send.at[q // 4], dec_in.at[d], sem, dec_sem.at[0], to_chip(q)).start()
    dec_in[0] = dec_send[chip // 4]

    for k in range(CHUNKS):
        hidden(2, k)
        down(2, k)
    for k in range(CHUNKS):
        arrived(sib_in.at[2, k], sib_sem.at[2, k])
        for n in range(4):
            blocks = [own[2, k, 4 * m + n] + sib_in[2, k, 4 * m + n].astype(F32) for m in range(4)]
            for g in range(4):
                turned = turn([b[8 * g : 8 * g + 8] for b in blocks])
                for a in range(4):
                    last[k, 4 * g + a, :, n * 128 : n * 128 + 128] = turned[a].astype(BF)
        sem = sending(last_in.at[k, pl.ds(1, NQ - 1)])
        for d in CHIP_STEPS:
            q = chip_at(d)
            remote(last.at[k, q], last_in.at[k, d], sem, last_sem.at[k], to_chip(q)).start()

    arrived(dec_in.at[pl.ds(1, NQ - 1)], dec_sem.at[0])
    quarter = lax.rem(chip, 4)

    def own_pair(block):
        block = jnp.where(quarter >= 2, pltpu.roll(block, 4, 0), block)
        return jnp.where(lax.rem(quarter, 2) == 1, pltpu.roll(block, 6, 0), block)

    for cb in range(NQ):
        step = lax.rem(z + 8 - cb // 2, 8) * 2 + lax.rem(yh + cb % 2, 2)
        both = dec_in[step].astype(F32)
        low, high = own_pair(both[0:8]), pltpu.roll(own_pair(both[8:16]), 2, 0)
        rows = jnp.where(lax.broadcasted_iota(jnp.int32, (8, 128), 0) < 2, low, high)
        dec_out[:, cb * 128 : cb * 128 + 128] = rows[0:4].astype(BF)

    results = []
    for k in range(CHUNKS):
        mine = rows_f[k, core, chip // 4]
        turned = turn([mine[:, m * 512 : m * 512 + 512] for m in range(4)])
        total = jnp.where(quarter == 0, turned[0], turned[1])
        total = jnp.where(quarter == 2, turned[2], total)
        total = jnp.where(quarter == 3, turned[3], total)
        results.append(total)
    for i, ref in enumerate(sent):
        remote(ref, ref, snd.at[i], snd.at[i], sibling).wait_send()
    for k in range(CHUNKS):
        arrived(last_in.at[k, pl.ds(1, NQ - 1)], last_sem.at[k])
        total = last[k, chip].astype(F32)
        for d in range(1, NQ):
            total = total + last_in[k, d].astype(F32)
        results[k] = (results[k] + total).astype(BF).astype(F32)
    even, odd = swap(results[0], results[1], 2)
    ev_out[:, 0:512] = even[0:4].astype(BF)
    ev_out[:, 512:1024] = odd[0:4].astype(BF)
    ev_out[:, 1024:1536] = even[4:8].astype(BF)
    ev_out[:, 1536:2048] = odd[4:8].astype(BF)


def on_device(
    beam_states, step_tokens, norm_gain, w_gate, w_up, w_down, prompt_table, kept_beams, prompt_ids
):
    vmem = pl.BlockSpec(memory_space=pltpu.VMEM)
    hbm = pl.BlockSpec(memory_space=pltpu.HBM)
    V, dma = pltpu.VMEM, pltpu.SemaphoreType.DMA
    LK = (LAYERS, CHUNKS)
    scratch = [
        V((4, WIDTH), BF), V((2, 4, WIDTH), BF), V((WIDTH,), BF), pltpu.SMEM((8,), jnp.int32), V((8, 16), jnp.int32),
        V((WIDTH, HID), BF), V((WIDTH, HID), BF), V((HID, WIDTH), BF), V((256, WIDTH), BF),
        V((128, WIDTH), BF),
        V((CHUNKS, 2, NQ, 8, 512), BF),
        V((*LK, 2, NQ, 32, 128), BF),
        V((64, WIDTH), BF),
        V((*LK, 8, 16, 1024), BF), V((*LK, 8, 16, 1024), BF),
        V((*LK, 8, 8, HID), BF), V((CHUNKS, 80, HID), BF),
        V((*LK, NQ, 32, 128), F32),
        V((*LK, NQ, 32, 128), BF), V((*LK, NQ, 32, 128), BF),
        V((2, CHUNKS, NQ, 32, 128), BF), V((2, CHUNKS, NQ, 32, 128), BF),
        V((NQ, 8, 128), BF), V((NQ, 8, 128), BF),
        V((NQ, 8, 128), F32), V((8, 8, 128), BF), V((8, 8, 128), BF),
        V((8, 8, 128), BF), V((NQ, 8, 8, 128), BF), V((NQ, 8, 128), BF),
        V((CHUNKS, 2, 4, 8, WIDTH), F32),
        V((4, 16, 128), BF), V((NQ, 16, 128), BF),
        V((CHUNKS, NQ, 8, 512), BF), V((CHUNKS, NQ, 8, 512), BF),
        dma((9,)), dma((48,)), dma((CHUNKS, NQ)), dma((CHUNKS,)), dma((NQ,)),
        dma((CHUNKS, NQ)), dma((CHUNKS,)), dma(LK), dma((*LK, 8)),
        dma(LK), dma(LK), dma((1,)), dma((1,)), dma((1,)), dma((1,)), dma((CHUNKS,)),
    ]
    return pl.pallas_call(
        kernel,
        out_shape=(jax.ShapeDtypeStruct((4, WIDTH), BF), jax.ShapeDtypeStruct((4, WIDTH), BF)),
        in_specs=[hbm] * 9,
        out_specs=(vmem, vmem),
        scratch_shapes=scratch,
        compiler_params=pltpu.CompilerParams(
            collective_id=0, has_side_effects=True, vmem_limit_bytes=56 * 2**20
        ),
        name="beam_steps",
    )(
        beam_states, step_tokens, norm_gain, kept_beams, prompt_ids,
        w_gate, w_up, w_down, prompt_table,
    )


def solution(mesh):
    return jax.shard_map(
        on_device,
        mesh=mesh,
        in_specs=(
            P("gy", "gx"),
            P(None, "gy", "gx"),
            P("gx"),
            P("gx", "gy"),
            P("gx", "gy"),
            P("gy", "gx"),
            P(None, "gx"),
            P(),
            P(),
        ),
        out_specs=(P("gy", "gx"), P("gy", "gx")),
        check_vma=False,
    )
```

```python
import jax
import jax.numpy as jnp
from jax import lax
from jax.experimental import pallas as pl
from jax.experimental.pallas import tpu as pltpu
from jax.sharding import PartitionSpec as P

D = 16384
EPS = 1e-05
BF, F32 = jnp.bfloat16, jnp.float32
NX, NY = 4, 2
NQ = 16
WIDTH = 2048
HID = 896
LAYERS, CHUNKS = 3, 2
MESH = pl.DeviceIdType.MESH

CHIP_STEPS = sorted(range(1, NQ), key=lambda d: -(min(d // 2, 8 - d // 2) + 2 * (d % 2)))
GX_STEPS = sorted(range(1, 8), key=lambda e: -(min(e % 4, 4 - e % 4) + e // 4))


def swap(a, b, rows):
    first = lax.rem(lax.broadcasted_iota(jnp.int32, a.shape, 0), 2 * rows) < rows
    return jnp.where(first, a, pltpu.roll(b, rows, 0)), jnp.where(first, pltpu.roll(a, 8 - rows, 0), b)


def turn(a):
    a0, a2 = swap(a[0], a[2], 4)
    a1, a3 = swap(a[1], a[3], 4)
    return (*swap(a0, a1, 2), *swap(a2, a3, 2))


def kernel(
    beam_hbm, tok_hbm, gain_hbm, kept_hbm, ids_hbm, wg_hbm, wu_hbm, wd_hbm, tab_hbm,
    dec_out, ev_out,
    beam, tok, gain, kept, ids, wg, wu, wd, tab, words, first, x, xs, part, part_in, hid, hid_mm,
    own, sib_out, sib_in, sums, sums_in, tok_out, tok_in,
    kp, kp_out, kp_in, ks, ks_in, pick_all, rows_f, dec_send, dec_in, last, last_in,
    load_sem, snd, first_sem, first_fwd, tok_sem, ag_sem, ag_fwd, rsx_sem, agx_sem,
    sib_sem, rsy_sem, kp_sem, ks_sem, pick_sem, dec_sem, last_sem,
):
    gx, gy = lax.axis_index("gx"), lax.axis_index("gy")
    px, pyl = lax.rem(gx, NX), gx // NX
    core, chip = lax.rem(gy, 2), gy // 2
    yh, z = lax.rem(chip, 2), chip // 2
    other = 1 - core
    sibling = (gx, chip * 2 + other)

    def chip_at(d):
        return lax.rem(z + d // 2, 8) * 2 + lax.rem(yh + d % 2, 2)

    def chip_from(d):
        return lax.rem(z + 8 - d // 2, 8) * 2 + lax.rem(yh + d % 2, 2)

    def gx_at(e):
        return lax.rem(pyl + e // 4, NY) * NX + lax.rem(px + e % 4, NX)

    def gx_from(e):
        return lax.rem(pyl + e // 4, NY) * NX + lax.rem(px + 4 - e % 4, NX)

    def to_chip(q):
        return (gx, q * 2 + core)

    def to_gx(p):
        return (p, gy)

    def remote(src, dst, send, recv, device):
        return pltpu.make_async_remote_copy(
            src_ref=src, dst_ref=dst, send_sem=send, recv_sem=recv, device_id=device, device_id_type=MESH
        )

    def arrived(ref, recv):
        remote(ref, ref, snd.at[0], recv, sibling).wait_recv()

    sent = []

    def sending(ref):
        sent.append(ref)
        return snd.at[len(sent) - 1]

    pairs = [
        (beam_hbm, beam), (tok_hbm, tok), (tab_hbm, tab), (ids_hbm, ids), (kept_hbm, kept), (gain_hbm, gain),
        (wg_hbm, wg), (wu_hbm, wu), (wd_hbm, wd),
    ]
    loads = [pltpu.make_async_copy(s, d, load_sem.at[i]) for i, (s, d) in enumerate(pairs)]
    for load in loads:
        load.start()

    barrier = pltpu.get_barrier_semaphore()
    for d in CHIP_STEPS:
        pl.semaphore_signal(barrier, inc=1, device_id=to_chip(chip_at(d)), device_id_type=MESH)
    for e in GX_STEPS:
        pl.semaphore_signal(barrier, inc=1, device_id=to_gx(gx_at(e)), device_id_type=MESH)
    pl.semaphore_signal(barrier, inc=1, device_id=sibling, device_id_type=MESH)

    loads[0].wait()
    loads[1].wait()
    mixed = (beam[...].astype(F32) + tok[0].astype(F32)).astype(BF).astype(F32)
    mixed = jnp.concatenate([mixed, mixed], axis=0)
    top = lax.broadcasted_iota(jnp.int32, (8, 512), 0) < 4
    even, odd = swap(
        jnp.where(top, mixed[:, 0:512], mixed[:, 1024:1536]), jnp.where(top, mixed[:, 512:1024], mixed[:, 1536:2048]), 2
    )
    first[0, core, chip] = even.astype(BF)
    first[1, core, chip] = odd.astype(BF)
    token = tok[1].astype(F32)
    token = jnp.concatenate([token, token], axis=0).astype(BF)
    for cb in range(NQ):
        tok_out[cb] = token[:, cb * 128 : cb * 128 + 128]

    pl.semaphore_wait(barrier, NQ - 1 + 7 + 1)

    forward = []
    for k in range(CHUNKS):
        piece = first.at[k, core, chip]
        sem = sending(first.at[k, 0, pl.ds(0, NQ - 1)])
        forward.append(sending(first.at[k, 0]))
        for d in CHIP_STEPS:
            remote(piece, piece, sem, first_sem.at[k, d], to_chip(chip_at(d))).start()
        remote(piece, piece, forward[k], first_fwd.at[k], sibling).start()
    sem = sending(tok_in.at[pl.ds(0, NQ - 1)])
    for d in CHIP_STEPS:
        remote(tok_out.at[chip_at(d)], tok_in.at[chip], sem, tok_sem.at[d], to_chip(chip_at(d))).start()
    tok_in[chip] = tok_out[chip]

    for load in loads[2:6]:
        load.wait()

    def row_of(shape, dim):
        t = lax.broadcasted_iota(jnp.int32, shape, dim)
        return 8 * (lax.rem(t, 32) // 2) + 4 * (lax.rem(t, 64) // 32) + 2 * (t // 64) + lax.rem(t, 2)

    of_beam = (row_of((128, 8), 0) // 16 == lax.broadcasted_iota(jnp.int32, (128, 8), 1)).astype(F32).astype(BF)
    beam_ids = jnp.dot(of_beam, ids[...].astype(F32).astype(BF), preferred_element_type=F32)
    place = lax.rem(row_of((128, 16), 0), 16) == lax.broadcasted_iota(jnp.int32, (128, 16), 1)
    row_ids = jnp.sum(jnp.where(place, beam_ids, 0.0), axis=1, keepdims=True)
    lookup = (row_ids == lax.broadcasted_iota(jnp.int32, (128, 256), 1).astype(F32)).astype(F32).astype(BF)
    for n in range(4):
        cols = slice(n * 512, n * 512 + 512)
        words[:, cols] = jnp.dot(lookup, tab[:, cols], preferred_element_type=F32).astype(BF)
    nth = lax.broadcasted_iota(jnp.int32, (16, 128), 0)
    kept_rows = jnp.full((16, 128), -1, jnp.int32)
    for n in range(8):
        kept_rows = jnp.where(nth == n, kept[n], kept_rows)
    picker = (kept_rows == row_of((16, 128), 1)).astype(F32).astype(BF)

    def prepare(layer, k):
        squares = []
        for h in range(2):
            total = jnp.zeros((32, 128), F32)
            for cb in range(NQ):
                v = x[layer, k, h, cb].astype(F32)
                total = total + v * v
                cols = slice(cb * 128, cb * 128 + 128)
                xs[h * 32 : h * 32 + 32, cols] = (v * gain[cols].astype(F32)[None, :]).astype(BF)
            squares.append(jnp.sum(total, axis=1, keepdims=True))
        whole = jnp.broadcast_to(jnp.concatenate(squares, axis=0), (64, 128))
        high = whole.astype(BF).astype(F32)
        both = jnp.concatenate([high.reshape(8, 8, 128), (whole - high).reshape(8, 8, 128)], axis=1)
        part[layer, k, :, :, HID:1024] = both.astype(BF)

    def up(layer, k):
        for n in range(HID // 128):
            cols = slice(n * 128, n * 128 + 128)
            weights = jnp.concatenate([wg[:, cols], wu[:, cols]], axis=1)
            y = jnp.dot(xs[...], weights, preferred_element_type=F32)
            both = jnp.concatenate([y[:, :128].reshape(8, 8, 128), y[:, 128:].reshape(8, 8, 128)], axis=1)
            part[layer, k, :, :, cols] = both.astype(BF)
        sem = sending(part_in.at[layer, k, pl.ds(1, 7)])
        for e in GX_STEPS:
            p = gx_at(e)
            remote(part.at[layer, k, p], part_in.at[layer, k, e], sem, rsx_sem.at[layer, k], to_gx(p)).start()

    def act(layer, k):
        arrived(part_in.at[layer, k, pl.ds(1, 7)], rsx_sem.at[layer, k])
        total = part[layer, k, gx].astype(F32)
        for e in range(1, 8):
            total = total + part_in[layer, k, e].astype(F32)
        squares = total[0:8, HID:1024] + total[8:16, HID:1024]
        scale = lax.rsqrt(squares / D + EPS)
        for n in range(HID // 128):
            cols = slice(n * 128, n * 128 + 128)
            g = scale * total[0:8, cols]
            u = scale * total[8:16, cols]
            hid[layer, k, gx, :, cols] = (g / (1.0 + jnp.exp(-g)) * u).astype(BF)
        piece = hid.at[layer, k, gx]
        sem = sending(hid.at[layer, k, pl.ds(0, 7)])
        for e in GX_STEPS:
            remote(piece, piece, sem, agx_sem.at[layer, k, e], to_gx(gx_at(e))).start()

    def hidden(layer, k):
        for e in reversed(GX_STEPS):
            arrived(hid.at[layer, k, gx_from(e)], agx_sem.at[layer, k, e])
        hid_mm[k, 0:64] = hid[layer, k].astype(F32).reshape(64, HID).astype(BF)

    def down(layer, k, with_kept=False):
        for n in range(8):
            rows = hid_mm[k] if with_kept else hid_mm[k, 0:64]
            y = jnp.dot(rows, wd[:, n * 256 : n * 256 + 256], preferred_element_type=F32)
            mine = jnp.where(core == 0, y[0:32], y[32:64])
            theirs = jnp.where(core == 0, y[32:64], y[0:32]).astype(BF)
            for m in range(2):
                own[layer, k, 2 * n + m] = mine[:, m * 128 : m * 128 + 128]
                sib_out[layer, k, 2 * n + m] = theirs[:, m * 128 : m * 128 + 128]
                if with_kept:
                    kp[2 * n + m] = y[64:72, m * 128 : m * 128 + 128]
        if with_kept:
            kp_out[...] = kp[pl.ds(8 * other, 8)].astype(BF)
            remote(kp_out, kp_in, sending(kp_out), kp_sem.at[0], sibling).start()
        sem = sending(sib_out.at[layer, k])
        remote(sib_out.at[layer, k], sib_in.at[layer, k], sem, sib_sem.at[layer, k], sibling).start()

    def scatter(layer, k):
        arrived(sib_in.at[layer, k], sib_sem.at[layer, k])
        sem = sending(sums_in.at[layer, k, pl.ds(1, NQ - 1)])
        for d in CHIP_STEPS:
            q = chip_at(d)
            sums[layer, k, q] = (own[layer, k, q] + sib_in[layer, k, q].astype(F32)).astype(BF)
            remote(sums.at[layer, k, q], sums_in.at[layer, k, d], sem, rsy_sem.at[layer, k], to_chip(q)).start()

    def new_state(layer, k):
        arrived(sums_in.at[layer, k, pl.ds(1, NQ - 1)], rsy_sem.at[layer, k])
        total = own[layer, k, chip] + sib_in[layer, k, chip].astype(F32)
        for d in range(1, NQ):
            total = total + sums_in[layer, k, d].astype(F32)
        return (x[layer, k, core, chip].astype(F32) + total).astype(BF).astype(F32)

    second_fwd = []

    def spread(k):
        state = new_state(0, k)
        if k == 0:
            for d in CHIP_STEPS:
                arrived(tok_in.at[chip_from(d)], tok_sem.at[d])
        pair = lax.broadcasted_iota(jnp.int32, (8, 128), 0) // 2
        groups = []
        for g in range(4):
            group = jnp.zeros((8, 128), F32)
            for a in range(4):
                t = tok_in[4 * g + a].astype(F32)
                group = jnp.where(pair == a, t if a % 2 == k else pltpu.roll(t, 2, 0), group)
            groups.append(group)
        x[1, k, core, chip] = (state + jnp.concatenate(groups, axis=0)).astype(BF)
        piece = x.at[1, k, core, chip]
        sem = sending(x.at[1, k, 0, pl.ds(0, NQ - 1)])
        second_fwd.append(sending(x.at[1, k, 0]))
        for d in CHIP_STEPS:
            remote(piece, piece, sem, ag_sem.at[k, d], to_chip(chip_at(d))).start()
        remote(piece, piece, second_fwd[k], ag_fwd.at[k], sibling).start()

    def collect(k):
        for d in reversed(CHIP_STEPS):
            piece = x.at[1, k, core, chip_from(d)]
            arrived(piece, ag_sem.at[k, d])
            remote(piece, piece, second_fwd[k], ag_fwd.at[k], sibling).start()
        arrived(x.at[1, k, other], ag_fwd.at[k])

    for k in range(CHUNKS):
        for d in reversed(CHIP_STEPS):
            piece = first.at[k, core, chip_from(d)]
            arrived(piece, first_sem.at[k, d])
            remote(piece, piece, forward[k], first_fwd.at[k], sibling).start()
        arrived(first.at[k, other], first_fwd.at[k])
        for h in range(2):
            for g in range(4):
                quarters = turn([first[k, h, 4 * g + a].astype(F32) for a in range(4)])
                for m in range(4):
                    rows_f[k, h, g, :, m * 512 : m * 512 + 512] = quarters[m]
            for cb in range(NQ):
                block = rows_f[k, h, :, :, cb * 128 : cb * 128 + 128]
                x[0, k, h, cb] = block.reshape(32, 128).astype(BF)
        prepare(0, k)
        if k == 0:
            loads[6].wait()
            loads[7].wait()
        up(0, k)
    for k in range(CHUNKS):
        act(0, k)
    loads[8].wait()
    for k in range(CHUNKS):
        hidden(0, k)
        down(0, k)
    for k in range(CHUNKS):
        scatter(0, k)
    for k in range(CHUNKS):
        spread(k)

    for k in range(CHUNKS):
        collect(k)
        prepare(1, k)
        up(1, k)
    for k in range(CHUNKS):
        act(1, k)
    kept_mixed = []
    for m in range(8):
        cb = 8 * core + m
        column = jnp.concatenate([x[1, k, h, cb] for k in range(CHUNKS) for h in range(2)], axis=0)
        kept_mixed.append(jnp.dot(picker, column, preferred_element_type=F32)[0:8])
    for k in range(CHUNKS):
        hidden(1, k)

    def pick_hidden(n, carry):
        cols = pl.ds(pl.multiple_of(n * 128, 128), 128)
        chosen = jnp.zeros((16, 128), F32)
        for k in range(CHUNKS):
            rows = picker[:, 64 * k : 64 * k + 64]
            chosen = chosen + jnp.dot(rows, hid_mm[k, 0:64, cols], preferred_element_type=F32)
        hid_mm[1, 64:80, cols] = chosen.astype(BF)
        return carry

    lax.fori_loop(0, HID // 128, pick_hidden, 0)
    down(1, 1, True)
    down(1, 0)

    arrived(kp_in, kp_sem.at[0])
    ks[...] = (kp[pl.ds(8 * core, 8)] + kp_in[...].astype(F32)).astype(BF)
    sem = sending(ks_in.at[pl.ds(1, NQ - 1)])
    for d in CHIP_STEPS:
        remote(ks, ks_in.at[d], sem, ks_sem.at[0], to_chip(chip_at(d))).start()
    arrived(ks_in.at[pl.ds(1, NQ - 1)], ks_sem.at[0])
    total = ks[...].astype(F32)
    for d in range(1, NQ):
        total = total + ks_in[d].astype(F32)
    for m in range(8):
        pick_all[8 * core + m] = (kept_mixed[m] + total[m]).astype(BF)
    half = pick_all.at[pl.ds(8 * core, 8)]
    remote(half, half, sending(half), pick_sem.at[0], sibling).start()
    arrived(half, pick_sem.at[0])

    upper = lax.broadcasted_iota(jnp.int32, (8, 128), 0) < 4
    for k in range(CHUNKS):
        for cb in range(NQ):
            cols = slice(cb * 128, cb * 128 + 128)
            chosen = pick_all[cb].astype(F32)
            chosen = jnp.concatenate(
                [jnp.where(upper, chosen[2 * g : 2 * g + 1], chosen[2 * g + 1 : 2 * g + 2]) for g in range(4)], axis=0
            )
            for h in range(2):
                at = 64 * k + 32 * h
                rows = (chosen + words[at : at + 32, cols].astype(F32)).astype(BF)
                x[2, k, h, cb] = rows
                rows_f[k, h, :, :, cols] = rows.astype(F32).reshape(4, 8, 128)
        prepare(2, k)
        up(2, k)

    for k in range(CHUNKS):
        scatter(1, k)
    for k in range(CHUNKS):
        act(2, k)
    for k in range(CHUNKS):
        state = new_state(1, k).reshape(4, 8, 128)
        dec_send[:, 8 * k : 8 * k + 8, :] = state.astype(BF)
    sem = sending(dec_in.at[pl.ds(1, NQ - 1)])
    for d in CHIP_STEPS:
        q = chip_at(d)
        remote(dec_send.at[q // 4], dec_in.at[d], sem, dec_sem.at[0], to_chip(q)).start()
    dec_in[0] = dec_send[chip // 4]

    for k in range(CHUNKS):
        hidden(2, k)
        down(2, k)
    for k in range(CHUNKS):
        arrived(sib_in.at[2, k], sib_sem.at[2, k])
        for n in range(4):
            blocks = [own[2, k, 4 * m + n] + sib_in[2, k, 4 * m + n].astype(F32) for m in range(4)]
            for g in range(4):
                turned = turn([b[8 * g : 8 * g + 8] for b in blocks])
                for a in range(4):
                    last[k, 4 * g + a, :, n * 128 : n * 128 + 128] = turned[a].astype(BF)
        sem = sending(last_in.at[k, pl.ds(1, NQ - 1)])
        for d in CHIP_STEPS:
            q = chip_at(d)
            remote(last.at[k, q], last_in.at[k, d], sem, last_sem.at[k], to_chip(q)).start()

    arrived(dec_in.at[pl.ds(1, NQ - 1)], dec_sem.at[0])
    quarter = lax.rem(chip, 4)

    def own_pair(block):
        block = jnp.where(quarter >= 2, pltpu.roll(block, 4, 0), block)
        return jnp.where(lax.rem(quarter, 2) == 1, pltpu.roll(block, 6, 0), block)

    for cb in range(NQ):
        step = lax.rem(z + 8 - cb // 2, 8) * 2 + lax.rem(yh + cb % 2, 2)
        both = dec_in[step].astype(F32)
        low, high = own_pair(both[0:8]), pltpu.roll(own_pair(both[8:16]), 2, 0)
        rows = jnp.where(lax.broadcasted_iota(jnp.int32, (8, 128), 0) < 2, low, high)
        dec_out[:, cb * 128 : cb * 128 + 128] = rows[0:4].astype(BF)

    results = []
    for k in range(CHUNKS):
        mine = rows_f[k, core, chip // 4]
        turned = turn([mine[:, m * 512 : m * 512 + 512] for m in range(4)])
        total = jnp.where(quarter == 0, turned[0], turned[1])
        total = jnp.where(quarter == 2, turned[2], total)
        total = jnp.where(quarter == 3, turned[3], total)
        results.append(total)
    for i, ref in enumerate(sent):
        remote(ref, ref, snd.at[i], snd.at[i], sibling).wait_send()
    for k in range(CHUNKS):
        arrived(last_in.at[k, pl.ds(1, NQ - 1)], last_sem.at[k])
        total = last[k, chip].astype(F32)
        for d in range(1, NQ):
            total = total + last_in[k, d].astype(F32)
        results[k] = (results[k] + total).astype(BF).astype(F32)
    even, odd = swap(results[0], results[1], 2)
    ev_out[:, 0:512] = even[0:4].astype(BF)
    ev_out[:, 512:1024] = odd[0:4].astype(BF)
    ev_out[:, 1024:1536] = even[4:8].astype(BF)
    ev_out[:, 1536:2048] = odd[4:8].astype(BF)


def on_device(
    beam_states, step_tokens, norm_gain, w_gate, w_up, w_down, prompt_table, kept_beams, prompt_ids
):
    vmem = pl.BlockSpec(memory_space=pltpu.VMEM)
    hbm = pl.BlockSpec(memory_space=pltpu.HBM)
    V, dma = pltpu.VMEM, pltpu.SemaphoreType.DMA
    LK = (LAYERS, CHUNKS)
    scratch = [
        V((4, WIDTH), BF), V((2, 4, WIDTH), BF), V((WIDTH,), BF), pltpu.SMEM((8,), jnp.int32), V((8, 16), jnp.int32),
        V((WIDTH, HID), BF), V((WIDTH, HID), BF), V((HID, WIDTH), BF), V((256, WIDTH), BF),
        V((128, WIDTH), BF),
        V((CHUNKS, 2, NQ, 8, 512), BF),
        V((*LK, 2, NQ, 32, 128), BF),
        V((64, WIDTH), BF),
        V((*LK, 8, 16, 1024), BF), V((*LK, 8, 16, 1024), BF),
        V((*LK, 8, 8, HID), BF), V((CHUNKS, 80, HID), BF),
        V((*LK, NQ, 32, 128), F32),
        V((*LK, NQ, 32, 128), BF), V((*LK, NQ, 32, 128), BF),
        V((2, CHUNKS, NQ, 32, 128), BF), V((2, CHUNKS, NQ, 32, 128), BF),
        V((NQ, 8, 128), BF), V((NQ, 8, 128), BF),
        V((NQ, 8, 128), F32), V((8, 8, 128), BF), V((8, 8, 128), BF),
        V((8, 8, 128), BF), V((NQ, 8, 8, 128), BF), V((NQ, 8, 128), BF),
        V((CHUNKS, 2, 4, 8, WIDTH), F32),
        V((4, 16, 128), BF), V((NQ, 16, 128), BF),
        V((CHUNKS, NQ, 8, 512), BF), V((CHUNKS, NQ, 8, 512), BF),
        dma((9,)), dma((48,)), dma((CHUNKS, NQ)), dma((CHUNKS,)), dma((NQ,)),
        dma((CHUNKS, NQ)), dma((CHUNKS,)), dma(LK), dma((*LK, 8)),
        dma(LK), dma(LK), dma((1,)), dma((1,)), dma((1,)), dma((1,)), dma((CHUNKS,)),
    ]
    return pl.pallas_call(
        kernel,
        out_shape=(jax.ShapeDtypeStruct((4, WIDTH), BF), jax.ShapeDtypeStruct((4, WIDTH), BF)),
        in_specs=[hbm] * 9,
        out_specs=(vmem, vmem),
        scratch_shapes=scratch,
        compiler_params=pltpu.CompilerParams(
            collective_id=0, has_side_effects=True, vmem_limit_bytes=56 * 2**20
        ),
        name="beam_steps",
    )(
        beam_states, step_tokens, norm_gain, kept_beams, prompt_ids,
        w_gate, w_up, w_down, prompt_table,
    )


def solution(mesh):
    return jax.shard_map(
        on_device,
        mesh=mesh,
        in_specs=(
            P("gy", "gx"),
            P(None, "gy", "gx"),
            P("gx"),
            P("gx", "gy"),
            P("gx", "gy"),
            P("gy", "gx"),
            P(None, "gx"),
            P(),
            P(),
        ),
        out_specs=(P("gy", "gx"), P("gy", "gx")),
        check_vma=False,
    )
```

```python
import jax
import jax.numpy as jnp
from jax import lax
from jax.experimental import pallas as pl
from jax.experimental.pallas import tpu as pltpu
from jax.sharding import PartitionSpec as P

D = 16384
EPS = 1e-05
BF, F32 = jnp.bfloat16, jnp.float32
NX, NY = 4, 2
NQ = 16
WIDTH = 2048
HID = 896
LAYERS, CHUNKS = 3, 2
MESH = pl.DeviceIdType.MESH

CHIP_STEPS = sorted(range(1, NQ), key=lambda d: -(min(d // 2, 8 - d // 2) + 2 * (d % 2)))
Z_STEPS = (4, 3, 5, 2, 6, 1, 7, 0)
BLOCK_PAIRS = (0, 2, 4, 6, 1, 3, 5, 7)
GX_STEPS = sorted(range(1, 8), key=lambda e: -(min(e % 4, 4 - e % 4) + e // 4))


def swap(a, b, rows):
    first = lax.rem(lax.broadcasted_iota(jnp.int32, a.shape, 0), 2 * rows) < rows
    return jnp.where(first, a, pltpu.roll(b, rows, 0)), jnp.where(first, pltpu.roll(a, 8 - rows, 0), b)


def turn(a):
    a0, a2 = swap(a[0], a[2], 4)
    a1, a3 = swap(a[1], a[3], 4)
    return (*swap(a0, a1, 2), *swap(a2, a3, 2))


def kernel(
    beam_hbm, tok_hbm, gain_hbm, kept_hbm, ids_hbm, wg_hbm, wu_hbm, wd_hbm, tab_hbm,
    dec_out, ev_out,
    beam, tok, gain, kept, ids, wg, wu, wd, tab, words, first, x, xs, part, part_in, hid, hid_mm,
    own, sib_out, sib_in, sums, sums_in, tok_out, tok_in,
    kp, kp_out, kp_in, ks, ks_in, pick_all, rows_f, tokens, last, last_in,
    load_sem, snd, first_sem, first_fwd, tok_sem, ag_sem, ag_fwd, rsx_sem, agx_sem,
    sib_sem, rsy_sem, kp_sem, ks_sem, pick_sem, last_sem,
):
    gx, gy = lax.axis_index("gx"), lax.axis_index("gy")
    px, pyl = lax.rem(gx, NX), gx // NX
    core, chip = lax.rem(gy, 2), gy // 2
    yh, z = lax.rem(chip, 2), chip // 2
    other = 1 - core
    sibling = (gx, chip * 2 + other)

    def chip_at(d):
        return lax.rem(z + d // 2, 8) * 2 + lax.rem(yh + d % 2, 2)

    def chip_from(d):
        return lax.rem(z + 8 - d // 2, 8) * 2 + lax.rem(yh + d % 2, 2)

    def gx_at(e):
        return lax.rem(pyl + e // 4, NY) * NX + lax.rem(px + e % 4, NX)

    def gx_from(e):
        return lax.rem(pyl + e // 4, NY) * NX + lax.rem(px + 4 - e % 4, NX)

    def to_chip(q):
        return (gx, q * 2 + core)

    def to_gx(p):
        return (p, gy)

    def remote(src, dst, send, recv, device):
        return pltpu.make_async_remote_copy(
            src_ref=src, dst_ref=dst, send_sem=send, recv_sem=recv, device_id=device, device_id_type=MESH
        )

    def arrived(ref, recv):
        remote(ref, ref, snd.at[0], recv, sibling).wait_recv()

    sent = []

    def sending(ref):
        sent.append(ref)
        return snd.at[len(sent) - 1]

    pairs = [
        (beam_hbm, beam), (tok_hbm, tok), (tab_hbm, tab), (ids_hbm, ids), (kept_hbm, kept), (gain_hbm, gain),
        (wg_hbm, wg), (wu_hbm, wu), (wd_hbm, wd),
    ]
    loads = [pltpu.make_async_copy(s, d, load_sem.at[i]) for i, (s, d) in enumerate(pairs)]
    for load in loads:
        load.start()

    barrier = pltpu.get_barrier_semaphore()
    for d in CHIP_STEPS:
        pl.semaphore_signal(barrier, inc=1, device_id=to_chip(chip_at(d)), device_id_type=MESH)
    for e in GX_STEPS:
        pl.semaphore_signal(barrier, inc=1, device_id=to_gx(gx_at(e)), device_id_type=MESH)
    pl.semaphore_signal(barrier, inc=1, device_id=sibling, device_id_type=MESH)

    loads[0].wait()
    loads[1].wait()
    mixed = (beam[...].astype(F32) + tok[0].astype(F32)).astype(BF).astype(F32)
    mixed = jnp.concatenate([mixed, mixed], axis=0)
    top = lax.broadcasted_iota(jnp.int32, (8, 512), 0) < 4
    even, odd = swap(
        jnp.where(top, mixed[:, 0:512], mixed[:, 1024:1536]), jnp.where(top, mixed[:, 512:1024], mixed[:, 1536:2048]), 2
    )
    first[0, core, chip] = even.astype(BF)
    first[1, core, chip] = odd.astype(BF)
    token = tok[1].astype(F32)
    token = jnp.concatenate([token, token], axis=0).astype(BF)
    for cb in range(NQ):
        tok_out[cb] = token[:, cb * 128 : cb * 128 + 128]

    pl.semaphore_wait(barrier, NQ - 1 + 7 + 1)

    forward = []
    for k in range(CHUNKS):
        piece = first.at[k, core, chip]
        sem = sending(first.at[k, 0, pl.ds(0, NQ - 1)])
        forward.append(sending(first.at[k, 0]))
        for d in CHIP_STEPS:
            remote(piece, piece, sem, first_sem.at[k, d], to_chip(chip_at(d))).start()
        remote(piece, piece, forward[k], first_fwd.at[k], sibling).start()
    sem = sending(tok_in.at[pl.ds(0, NQ - 1)])
    for d in CHIP_STEPS:
        remote(tok_out.at[chip_at(d)], tok_in.at[chip], sem, tok_sem.at[d], to_chip(chip_at(d))).start()
    tok_in[chip] = tok_out[chip]

    for load in loads[2:6]:
        load.wait()

    def row_of(shape, dim):
        t = lax.broadcasted_iota(jnp.int32, shape, dim)
        return 8 * (lax.rem(t, 32) // 2) + 4 * (lax.rem(t, 64) // 32) + 2 * (t // 64) + lax.rem(t, 2)

    of_beam = (row_of((128, 8), 0) // 16 == lax.broadcasted_iota(jnp.int32, (128, 8), 1)).astype(F32).astype(BF)
    beam_ids = jnp.dot(of_beam, ids[...].astype(F32).astype(BF), preferred_element_type=F32)
    place = lax.rem(row_of((128, 16), 0), 16) == lax.broadcasted_iota(jnp.int32, (128, 16), 1)
    row_ids = jnp.sum(jnp.where(place, beam_ids, 0.0), axis=1, keepdims=True)
    lookup = (row_ids == lax.broadcasted_iota(jnp.int32, (128, 256), 1).astype(F32)).astype(F32).astype(BF)
    for n in range(4):
        cols = slice(n * 512, n * 512 + 512)
        words[:, cols] = jnp.dot(lookup, tab[:, cols], preferred_element_type=F32).astype(BF)
    nth = lax.broadcasted_iota(jnp.int32, (16, 128), 0)
    kept_rows = jnp.full((16, 128), -1, jnp.int32)
    for n in range(8):
        kept_rows = jnp.where(nth == n, kept[n], kept_rows)
    picker = (kept_rows == row_of((16, 128), 1)).astype(F32).astype(BF)

    def prepare(layer, k):
        squares = []
        for h in range(2):
            total = jnp.zeros((32, 128), F32)
            for cb in range(NQ):
                v = x[layer, k, h, cb].astype(F32)
                total = total + v * v
                cols = slice(cb * 128, cb * 128 + 128)
                xs[h * 32 : h * 32 + 32, cols] = (v * gain[cols].astype(F32)[None, :]).astype(BF)
            squares.append(jnp.sum(total, axis=1, keepdims=True))
        whole = jnp.broadcast_to(jnp.concatenate(squares, axis=0), (64, 128))
        high = whole.astype(BF).astype(F32)
        both = jnp.concatenate([high.reshape(8, 8, 128), (whole - high).reshape(8, 8, 128)], axis=1)
        part[layer, k, :, :, HID:1024] = both.astype(BF)

    def up(layer, k):
        for n in range(HID // 128):
            cols = slice(n * 128, n * 128 + 128)
            weights = jnp.concatenate([wg[:, cols], wu[:, cols]], axis=1)
            y = jnp.dot(xs[...], weights, preferred_element_type=F32)
            both = jnp.concatenate([y[:, :128].reshape(8, 8, 128), y[:, 128:].reshape(8, 8, 128)], axis=1)
            part[layer, k, :, :, cols] = both.astype(BF)
        sem = sending(part_in.at[layer, k, pl.ds(1, 7)])
        for e in GX_STEPS:
            p = gx_at(e)
            remote(part.at[layer, k, p], part_in.at[layer, k, e], sem, rsx_sem.at[layer, k], to_gx(p)).start()

    def act(layer, k):
        arrived(part_in.at[layer, k, pl.ds(1, 7)], rsx_sem.at[layer, k])
        total = part[layer, k, gx].astype(F32)
        for e in range(1, 8):
            total = total + part_in[layer, k, e].astype(F32)
        squares = total[0:8, HID:1024] + total[8:16, HID:1024]
        scale = lax.rsqrt(squares / D + EPS)
        for n in range(HID // 128):
            cols = slice(n * 128, n * 128 + 128)
            g = scale * total[0:8, cols]
            u = scale * total[8:16, cols]
            hid[layer, k, gx, :, cols] = (g / (1.0 + jnp.exp(-g)) * u).astype(BF)
        piece = hid.at[layer, k, gx]
        sem = sending(hid.at[layer, k, pl.ds(0, 7)])
        for e in GX_STEPS:
            remote(piece, piece, sem, agx_sem.at[layer, k, e], to_gx(gx_at(e))).start()

    def hidden(layer, k):
        for e in reversed(GX_STEPS):
            arrived(hid.at[layer, k, gx_from(e)], agx_sem.at[layer, k, e])
        hid_mm[k, 0:64] = hid[layer, k].astype(F32).reshape(64, HID).astype(BF)

    def down(layer, k, with_kept=False):
        for j in range(8):
            pair = lax.rem(z + Z_STEPS[j], 8) if layer == 0 else BLOCK_PAIRS[j]
            rows = hid_mm[k] if with_kept else hid_mm[k, 0:64]
            cols = pl.ds(pl.multiple_of(pair * 256, 256), 256) if layer == 0 else slice(pair * 256, pair * 256 + 256)
            y = jnp.dot(rows, wd[:, cols], preferred_element_type=F32)
            mine = jnp.where(core == 0, y[0:32], y[32:64])
            theirs = jnp.where(core == 0, y[32:64], y[0:32]).astype(BF)
            for m in range(2):
                own[layer, k, 2 * j + m] = mine[:, m * 128 : m * 128 + 128]
                sib_out[layer, k, 2 * j + m] = theirs[:, m * 128 : m * 128 + 128]
                if with_kept:
                    kp[2 * pair + m] = y[64:72, m * 128 : m * 128 + 128]
            if j % 4 == 3 and not with_kept:
                share_sums(layer, k, j // 4)
        if with_kept:
            kp_out[...] = kp[pl.ds(8 * other, 8)].astype(BF)
            remote(kp_out, kp_in, sending(kp_out), kp_sem.at[0], sibling).start()
            for half in range(2):
                share_sums(layer, k, half)

    def share_sums(layer, k, half):
        at = pl.ds(8 * half, 8)
        sem = sending(sib_out.at[layer, k, at])
        remote(sib_out.at[layer, k, at], sib_in.at[layer, k, at], sem, sib_sem.at[layer, k, half], sibling).start()

    def shared(layer, k, half):
        arrived(sib_in.at[layer, k, pl.ds(8 * half, 8)], sib_sem.at[layer, k, half])

    def scatter(k):
        sem = sending(sums_in.at[k, pl.ds(1, NQ - 1)])
        for j in range(8):
            if j % 4 == 0:
                shared(0, k, j // 4)
            for dyh in (1, 0):
                d = 2 * Z_STEPS[j] + dyh
                if d == 0:
                    continue
                at = 2 * j + lax.rem(yh + dyh, 2)
                sums[k, d] = (own[0, k, at] + sib_in[0, k, at].astype(F32)).astype(BF)
                remote(sums.at[k, d], sums_in.at[k, d], sem, rsy_sem.at[k], to_chip(chip_at(d))).start()

    def scatter_rows(layer, k):
        for n in range(4):
            if n % 2 == 0:
                shared(layer, k, n // 2)
            blocks = []
            for m in range(4):
                at = 2 * BLOCK_PAIRS.index((4 * m + n) // 2) + n % 2
                blocks.append(own[layer, k, at] + sib_in[layer, k, at].astype(F32))
            for g in range(4):
                turned = turn([b[8 * g : 8 * g + 8] for b in blocks])
                for a in range(4):
                    last[layer - 1, k, 4 * g + a, :, n * 128 : n * 128 + 128] = turned[a].astype(BF)
        sem = sending(last_in.at[layer - 1, k, pl.ds(1, NQ - 1)])
        for d in CHIP_STEPS:
            q = chip_at(d)
            landing = last_in.at[layer - 1, k, d]
            remote(last.at[layer - 1, k, q], landing, sem, last_sem.at[layer - 1, k], to_chip(q)).start()

    quarter = lax.rem(chip, 4)

    def own_rows(block):
        turned = turn([block[:, m * 512 : m * 512 + 512] for m in range(4)])
        rows = jnp.where(quarter == 0, turned[0], turned[1])
        rows = jnp.where(quarter == 2, turned[2], rows)
        return jnp.where(quarter == 3, turned[3], rows)

    def add_sums(layer, k, rows):
        arrived(last_in.at[layer - 1, k, pl.ds(1, NQ - 1)], last_sem.at[layer - 1, k])
        total = last[layer - 1, k, chip].astype(F32)
        for d in range(1, NQ):
            total = total + last_in[layer - 1, k, d].astype(F32)
        return (rows + total).astype(BF).astype(F32)

    def write_rows(out, pair0, pair1):
        even, odd = swap(pair0, pair1, 2)
        out[:, 0:512] = even[0:4].astype(BF)
        out[:, 512:1024] = odd[0:4].astype(BF)
        out[:, 1024:1536] = even[4:8].astype(BF)
        out[:, 1536:2048] = odd[4:8].astype(BF)

    def new_state(k):
        arrived(sums_in.at[k, pl.ds(1, NQ - 1)], rsy_sem.at[k])
        total = own[0, k, 14 + yh] + sib_in[0, k, 14 + yh].astype(F32)
        for d in range(1, NQ):
            total = total + sums_in[k, d].astype(F32)
        return (x[0, k, core, chip].astype(F32) + total).astype(BF).astype(F32)

    second_fwd = []

    def take_tokens():
        for d in CHIP_STEPS:
            arrived(tok_in.at[chip_from(d)], tok_sem.at[d])
        pair = lax.broadcasted_iota(jnp.int32, (8, 128), 0) // 2
        for k in range(CHUNKS):
            for g in range(4):
                group = jnp.zeros((8, 128), F32)
                for a in range(4):
                    t = tok_in[4 * g + a].astype(F32)
                    group = jnp.where(pair == a, t if a % 2 == k else pltpu.roll(t, 2, 0), group)
                tokens[k, 8 * g : 8 * g + 8] = group

    def spread(k):
        x[1, k, core, chip] = (new_state(k) + tokens[k]).astype(BF)
        piece = x.at[1, k, core, chip]
        sem = sending(x.at[1, k, 0, pl.ds(0, NQ - 1)])
        second_fwd.append(sending(x.at[1, k, 0]))
        for d in CHIP_STEPS:
            remote(piece, piece, sem, ag_sem.at[k, d], to_chip(chip_at(d))).start()
        remote(piece, piece, second_fwd[k], ag_fwd.at[k], sibling).start()

    def collect(k):
        for d in reversed(CHIP_STEPS):
            piece = x.at[1, k, core, chip_from(d)]
            arrived(piece, ag_sem.at[k, d])
            remote(piece, piece, second_fwd[k], ag_fwd.at[k], sibling).start()
        arrived(x.at[1, k, other], ag_fwd.at[k])

    for k in range(CHUNKS):
        for d in reversed(CHIP_STEPS):
            piece = first.at[k, core, chip_from(d)]
            arrived(piece, first_sem.at[k, d])
            remote(piece, piece, forward[k], first_fwd.at[k], sibling).start()
        arrived(first.at[k, other], first_fwd.at[k])
        for h in range(2):
            for g in range(4):
                quarters = turn([first[k, h, 4 * g + a].astype(F32) for a in range(4)])
                for m in range(4):
                    rows_f[k, h, g, :, m * 512 : m * 512 + 512] = quarters[m]
            for cb in range(NQ):
                block = rows_f[k, h, :, :, cb * 128 : cb * 128 + 128]
                x[0, k, h, cb] = block.reshape(32, 128).astype(BF)
        prepare(0, k)
        if k == 0:
            loads[6].wait()
            loads[7].wait()
        up(0, k)
    for k in range(CHUNKS):
        act(0, k)
    take_tokens()
    loads[8].wait()
    for k in range(CHUNKS):
        hidden(0, k)
        down(0, k)
    for k in range(CHUNKS):
        scatter(k)
    for k in range(CHUNKS):
        spread(k)

    for k in range(CHUNKS):
        collect(k)
        prepare(1, k)
        up(1, k)
    for k in range(CHUNKS):
        act(1, k)
    kept_mixed = []
    for m in range(8):
        cb = 8 * core + m
        column = jnp.concatenate([x[1, k, h, cb] for k in range(CHUNKS) for h in range(2)], axis=0)
        kept_mixed.append(jnp.dot(picker, column, preferred_element_type=F32)[0:8])
    for k in range(CHUNKS):
        hidden(1, k)

    def pick_hidden(n, carry):
        cols = pl.ds(pl.multiple_of(n * 128, 128), 128)
        chosen = jnp.zeros((16, 128), F32)
        for k in range(CHUNKS):
            rows = picker[:, 64 * k : 64 * k + 64]
            chosen = chosen + jnp.dot(rows, hid_mm[k, 0:64, cols], preferred_element_type=F32)
        hid_mm[1, 64:80, cols] = chosen.astype(BF)
        return carry

    lax.fori_loop(0, HID // 128, pick_hidden, 0)
    down(1, 1, True)
    down(1, 0)

    arrived(kp_in, kp_sem.at[0])
    ks[...] = (kp[pl.ds(8 * core, 8)] + kp_in[...].astype(F32)).astype(BF)
    sem = sending(ks_in.at[pl.ds(1, NQ - 1)])
    for d in CHIP_STEPS:
        remote(ks, ks_in.at[d], sem, ks_sem.at[0], to_chip(chip_at(d))).start()
    arrived(ks_in.at[pl.ds(1, NQ - 1)], ks_sem.at[0])
    total = ks[...].astype(F32)
    for d in range(1, NQ):
        total = total + ks_in[d].astype(F32)
    for m in range(8):
        pick_all[8 * core + m] = (kept_mixed[m] + total[m]).astype(BF)
    half = pick_all.at[pl.ds(8 * core, 8)]
    remote(half, half, sending(half), pick_sem.at[0], sibling).start()
    arrived(half, pick_sem.at[0])

    upper = lax.broadcasted_iota(jnp.int32, (8, 128), 0) < 4
    for k in range(CHUNKS):
        for cb in range(NQ):
            cols = slice(cb * 128, cb * 128 + 128)
            chosen = pick_all[cb].astype(F32)
            chosen = jnp.concatenate(
                [jnp.where(upper, chosen[2 * g : 2 * g + 1], chosen[2 * g + 1 : 2 * g + 2]) for g in range(4)], axis=0
            )
            for h in range(2):
                at = 64 * k + 32 * h
                rows = (chosen + words[at : at + 32, cols].astype(F32)).astype(BF)
                x[2, k, h, cb] = rows
                rows_f[k, h, :, :, cols] = rows.astype(F32).reshape(4, 8, 128)
        prepare(2, k)
        up(2, k)

    for k in range(CHUNKS):
        scatter_rows(1, k)
    for k in range(CHUNKS):
        act(2, k)
    for k in range(CHUNKS):
        hidden(2, k)
        down(2, k)
    for k in range(CHUNKS):
        scatter_rows(2, k)

    group = chip // 4
    results = []
    for k in range(CHUNKS):
        columns = []
        for cb in range(NQ):
            rows = x[1, k, core, cb].astype(F32)
            eight = jnp.where(group == 0, rows[0:8], rows[8:16])
            eight = jnp.where(group == 2, rows[16:24], eight)
            columns.append(jnp.where(group == 3, rows[24:32], eight))
        results.append(add_sums(1, k, own_rows(jnp.concatenate(columns, axis=1))))
    write_rows(dec_out, *results)
    residuals = [own_rows(rows_f[k, core, group]) for k in range(CHUNKS)]
    for i, ref in enumerate(sent):
        remote(ref, ref, snd.at[i], snd.at[i], sibling).wait_send()
    write_rows(ev_out, *[add_sums(2, k, residuals[k]) for k in range(CHUNKS)])


def on_device(
    beam_states, step_tokens, norm_gain, w_gate, w_up, w_down, prompt_table, kept_beams, prompt_ids
):
    vmem = pl.BlockSpec(memory_space=pltpu.VMEM)
    hbm = pl.BlockSpec(memory_space=pltpu.HBM)
    V, dma = pltpu.VMEM, pltpu.SemaphoreType.DMA
    LK = (LAYERS, CHUNKS)
    scratch = [
        V((4, WIDTH), BF), V((2, 4, WIDTH), BF), V((WIDTH,), BF), pltpu.SMEM((8,), jnp.int32), V((8, 16), jnp.int32),
        V((WIDTH, HID), BF), V((WIDTH, HID), BF), V((HID, WIDTH), BF), V((256, WIDTH), BF),
        V((128, WIDTH), BF),
        V((CHUNKS, 2, NQ, 8, 512), BF),
        V((*LK, 2, NQ, 32, 128), BF),
        V((64, WIDTH), BF),
        V((*LK, 8, 16, 1024), BF), V((*LK, 8, 16, 1024), BF),
        V((*LK, 8, 8, HID), BF), V((CHUNKS, 80, HID), BF),
        V((*LK, NQ, 32, 128), F32),
        V((*LK, NQ, 32, 128), BF), V((*LK, NQ, 32, 128), BF),
        V((CHUNKS, NQ, 32, 128), BF), V((CHUNKS, NQ, 32, 128), BF),
        V((NQ, 8, 128), BF), V((NQ, 8, 128), BF),
        V((NQ, 8, 128), F32), V((8, 8, 128), BF), V((8, 8, 128), BF),
        V((8, 8, 128), BF), V((NQ, 8, 8, 128), BF), V((NQ, 8, 128), BF),
        V((CHUNKS, 2, 4, 8, WIDTH), F32),
        V((CHUNKS, 32, 128), F32),
        V((2, CHUNKS, NQ, 8, 512), BF), V((2, CHUNKS, NQ, 8, 512), BF),
        dma((9,)), dma((48,)), dma((CHUNKS, NQ)), dma((CHUNKS,)), dma((NQ,)),
        dma((CHUNKS, NQ)), dma((CHUNKS,)), dma(LK), dma((*LK, 8)),
        dma((*LK, 2)), dma((CHUNKS,)), dma((1,)), dma((1,)), dma((1,)), dma((2, CHUNKS)),
    ]
    return pl.pallas_call(
        kernel,
        out_shape=(jax.ShapeDtypeStruct((4, WIDTH), BF), jax.ShapeDtypeStruct((4, WIDTH), BF)),
        in_specs=[hbm] * 9,
        out_specs=(vmem, vmem),
        scratch_shapes=scratch,
        compiler_params=pltpu.CompilerParams(
            collective_id=0, has_side_effects=True, vmem_limit_bytes=56 * 2**20
        ),
        name="beam_steps",
    )(
        beam_states, step_tokens, norm_gain, kept_beams, prompt_ids,
        w_gate, w_up, w_down, prompt_table,
    )


def solution(mesh):
    return jax.shard_map(
        on_device,
        mesh=mesh,
        in_specs=(
            P("gy", "gx"),
            P(None, "gy", "gx"),
            P("gx"),
            P("gx", "gy"),
            P("gx", "gy"),
            P("gy", "gx"),
            P(None, "gx"),
            P(),
            P(),
        ),
        out_specs=(P("gy", "gx"), P("gy", "gx")),
        check_vma=False,
    )
```

```python
import jax
import jax.numpy as jnp
from jax import lax
from jax.experimental import pallas as pl
from jax.experimental.pallas import tpu as pltpu
from jax.sharding import PartitionSpec as P

D = 16384
EPS = 1e-05
BF, F32 = jnp.bfloat16, jnp.float32
NX, NY = 4, 2
NQ = 16
WIDTH = 2048
HID = 896
LAYERS, CHUNKS = 3, 2
MESH = pl.DeviceIdType.MESH

CHIP_STEPS = sorted(range(1, NQ), key=lambda d: -(min(d // 2, 8 - d // 2) + 2 * (d % 2)))
Z_STEPS = (4, 3, 5, 2, 6, 1, 7, 0)
BLOCK_PAIRS = (0, 2, 4, 6, 1, 3, 5, 7)
GX_STEPS = sorted(range(1, 8), key=lambda e: (-min(e % 4, 4 - e % 4), -(e // 4)))
NEAR_FIRST = CHIP_STEPS[::-1]


def swap(a, b, rows):
    first = lax.rem(lax.broadcasted_iota(jnp.int32, a.shape, 0), 2 * rows) < rows
    return jnp.where(first, a, pltpu.roll(b, rows, 0)), jnp.where(first, pltpu.roll(a, 8 - rows, 0), b)


def turn(a):
    a0, a2 = swap(a[0], a[2], 4)
    a1, a3 = swap(a[1], a[3], 4)
    return (*swap(a0, a1, 2), *swap(a2, a3, 2))


def kernel(
    beam_hbm, tok_hbm, gain_hbm, kept_hbm, ids_hbm, wg_hbm, wu_hbm, wd_hbm, tab_hbm,
    dec_out, ev_out,
    beam, tok, gain, kept, ids, wg, wu, wd, tab, words, first, x, xs, part, part_in, hid, hid_mm,
    own, sib_out, sib_in, sums, sums_in, tok_out, tok_in,
    kp, kp_out, kp_in, ks, ks_in, pick_all, rows_f, tokens, last, last_in, z_in, joined, pair_out, pair_in,
    load_sem, snd, first_sem, first_fwd, tok_sem, ag_sem, ag_fwd, rsx_sem, agx_sem,
    sib_sem, rsy_sem, kp_sem, ks_sem, pick_sem, last_sem, z_sem, pair_sem,
):
    gx, gy = lax.axis_index("gx"), lax.axis_index("gy")
    px, pyl = lax.rem(gx, NX), gx // NX
    core, chip = lax.rem(gy, 2), gy // 2
    yh, z = lax.rem(chip, 2), chip // 2
    other = 1 - core
    sibling = (gx, chip * 2 + other)

    def chip_at(d):
        return lax.rem(z + d // 2, 8) * 2 + lax.rem(yh + d % 2, 2)

    def chip_from(d):
        return lax.rem(z + 8 - d // 2, 8) * 2 + lax.rem(yh + d % 2, 2)

    def gx_at(e):
        return lax.rem(pyl + e // 4, NY) * NX + lax.rem(px + e % 4, NX)

    def gx_from(e):
        return lax.rem(pyl + e // 4, NY) * NX + lax.rem(px + 4 - e % 4, NX)

    def to_chip(q):
        return (gx, q * 2 + core)

    def to_gx(p):
        return (p, gy)

    def remote(src, dst, send, recv, device):
        return pltpu.make_async_remote_copy(
            src_ref=src, dst_ref=dst, send_sem=send, recv_sem=recv, device_id=device, device_id_type=MESH
        )

    def arrived(ref, recv):
        remote(ref, ref, snd.at[0], recv, sibling).wait_recv()

    sent = []

    def sending(ref):
        sent.append(ref)
        return snd.at[len(sent) - 1]

    pairs = [
        (beam_hbm, beam), (tok_hbm, tok), (tab_hbm, tab), (ids_hbm, ids), (kept_hbm, kept), (gain_hbm, gain),
        (wg_hbm, wg), (wu_hbm, wu), (wd_hbm, wd),
    ]
    loads = [pltpu.make_async_copy(s, d, load_sem.at[i]) for i, (s, d) in enumerate(pairs)]
    for load in loads:
        load.start()

    barrier = pltpu.get_barrier_semaphore()
    for d in CHIP_STEPS:
        pl.semaphore_signal(barrier, inc=1, device_id=to_chip(chip_at(d)), device_id_type=MESH)
    for e in GX_STEPS:
        pl.semaphore_signal(barrier, inc=1, device_id=to_gx(gx_at(e)), device_id_type=MESH)
    pl.semaphore_signal(barrier, inc=1, device_id=sibling, device_id_type=MESH)

    loads[0].wait()
    loads[1].wait()
    mixed = (beam[...].astype(F32) + tok[0].astype(F32)).astype(BF).astype(F32)
    mixed = jnp.concatenate([mixed, mixed], axis=0)
    top = lax.broadcasted_iota(jnp.int32, (8, 512), 0) < 4
    even, odd = swap(
        jnp.where(top, mixed[:, 0:512], mixed[:, 1024:1536]), jnp.where(top, mixed[:, 512:1024], mixed[:, 1536:2048]), 2
    )
    first[0, core, chip] = even.astype(BF)
    first[1, core, chip] = odd.astype(BF)
    token = tok[1].astype(F32)
    token = jnp.concatenate([token, token], axis=0).astype(BF)
    for cb in range(NQ):
        tok_out[cb] = token[:, cb * 128 : cb * 128 + 128]

    pl.semaphore_wait(barrier, NQ - 1 + 7 + 1)

    forward = []
    for k in range(CHUNKS):
        piece = first.at[k, core, chip]
        sem = sending(first.at[k, 0, pl.ds(0, NQ - 1)])
        forward.append(sending(first.at[k, 0]))
        for d in CHIP_STEPS:
            remote(piece, piece, sem, first_sem.at[k, d], to_chip(chip_at(d))).start()
        remote(piece, piece, forward[k], first_fwd.at[k], sibling).start()
    sem = sending(tok_in.at[pl.ds(0, NQ - 1)])
    for d in CHIP_STEPS:
        remote(tok_out.at[chip_at(d)], tok_in.at[chip], sem, tok_sem.at[d], to_chip(chip_at(d))).start()
    tok_in[chip] = tok_out[chip]

    for load in loads[2:6]:
        load.wait()

    def row_of(shape, dim):
        t = lax.broadcasted_iota(jnp.int32, shape, dim)
        return 8 * (lax.rem(t, 32) // 2) + 4 * (lax.rem(t, 64) // 32) + 2 * (t // 64) + lax.rem(t, 2)

    of_beam = (row_of((128, 8), 0) // 16 == lax.broadcasted_iota(jnp.int32, (128, 8), 1)).astype(F32).astype(BF)
    beam_ids = jnp.dot(of_beam, ids[...].astype(F32).astype(BF), preferred_element_type=F32)
    place = lax.rem(row_of((128, 16), 0), 16) == lax.broadcasted_iota(jnp.int32, (128, 16), 1)
    row_ids = jnp.sum(jnp.where(place, beam_ids, 0.0), axis=1, keepdims=True)
    lookup = (row_ids == lax.broadcasted_iota(jnp.int32, (128, 256), 1).astype(F32)).astype(F32).astype(BF)
    for n in range(4):
        cols = slice(n * 512, n * 512 + 512)
        words[:, cols] = jnp.dot(lookup, tab[:, cols], preferred_element_type=F32).astype(BF)
    nth = lax.broadcasted_iota(jnp.int32, (16, 128), 0)
    kept_rows = jnp.full((16, 128), -1, jnp.int32)
    for n in range(8):
        kept_rows = jnp.where(nth == n, kept[n], kept_rows)
    picker = (kept_rows == row_of((16, 128), 1)).astype(F32).astype(BF)

    def prepare(layer, k):
        squares = []
        for h in range(2):
            total = jnp.zeros((32, 128), F32)
            for cb in range(NQ):
                v = x[layer, k, h, cb].astype(F32)
                total = total + v * v
                cols = slice(cb * 128, cb * 128 + 128)
                xs[h * 32 : h * 32 + 32, cols] = (v * gain[cols].astype(F32)[None, :]).astype(BF)
            squares.append(jnp.sum(total, axis=1, keepdims=True))
        whole = jnp.broadcast_to(jnp.concatenate(squares, axis=0), (64, 128))
        high = whole.astype(BF).astype(F32)
        both = jnp.concatenate([high.reshape(8, 8, 128), (whole - high).reshape(8, 8, 128)], axis=1)
        part[layer, k, :, :, HID:1024] = both.astype(BF)

    def up(layer, k):
        for n in range(HID // 128):
            cols = slice(n * 128, n * 128 + 128)
            weights = jnp.concatenate([wg[:, cols], wu[:, cols]], axis=1)
            y = jnp.dot(xs[...], weights, preferred_element_type=F32)
            both = jnp.concatenate([y[:, :128].reshape(8, 8, 128), y[:, 128:].reshape(8, 8, 128)], axis=1)
            part[layer, k, :, :, cols] = both.astype(BF)
        sem = sending(part_in.at[layer, k, pl.ds(1, 7)])
        for e in GX_STEPS:
            p = gx_at(e)
            remote(part.at[layer, k, p], part_in.at[layer, k, e], sem, rsx_sem.at[layer, k], to_gx(p)).start()

    def act(layer, k):
        arrived(part_in.at[layer, k, pl.ds(1, 7)], rsx_sem.at[layer, k])
        total = part[layer, k, gx].astype(F32)
        for e in range(1, 8):
            total = total + part_in[layer, k, e].astype(F32)
        squares = total[0:8, HID:1024] + total[8:16, HID:1024]
        scale = lax.rsqrt(squares / D + EPS)
        for n in range(HID // 128):
            cols = slice(n * 128, n * 128 + 128)
            g = scale * total[0:8, cols]
            u = scale * total[8:16, cols]
            hid[layer, k, gx, :, cols] = (g / (1.0 + jnp.exp(-g)) * u).astype(BF)
        piece = hid.at[layer, k, gx]
        sem = sending(hid.at[layer, k, pl.ds(0, 7)])
        for e in GX_STEPS:
            remote(piece, piece, sem, agx_sem.at[layer, k, e], to_gx(gx_at(e))).start()

    def hidden(layer, k):
        for e in reversed(GX_STEPS):
            arrived(hid.at[layer, k, gx_from(e)], agx_sem.at[layer, k, e])
        hid_mm[k, 0:64] = hid[layer, k].astype(F32).reshape(64, HID).astype(BF)

    def down(layer, k, with_kept=False):
        for j in range(8):
            pair = lax.rem(z + Z_STEPS[j], 8) if layer == 0 else BLOCK_PAIRS[j]
            rows = hid_mm[k] if with_kept else hid_mm[k, 0:64]
            cols = pl.ds(pl.multiple_of(pair * 256, 256), 256) if layer == 0 else slice(pair * 256, pair * 256 + 256)
            y = jnp.dot(rows, wd[:, cols], preferred_element_type=F32)
            mine = jnp.where(core == 0, y[0:32], y[32:64])
            theirs = jnp.where(core == 0, y[32:64], y[0:32]).astype(BF)
            for m in range(2):
                own[layer, k, 2 * j + m] = mine[:, m * 128 : m * 128 + 128]
                sib_out[layer, k, 2 * j + m] = theirs[:, m * 128 : m * 128 + 128]
                if with_kept:
                    kp[2 * pair + m] = y[64:72, m * 128 : m * 128 + 128]
            if j % 4 == 3 and not with_kept:
                share_sums(layer, k, j // 4)
        if with_kept:
            kp_out[...] = kp[pl.ds(8 * other, 8)].astype(BF)
            remote(kp_out, kp_in, sending(kp_out), kp_sem.at[0], sibling).start()
            for half in range(2):
                share_sums(layer, k, half)

    def share_sums(layer, k, half):
        at = pl.ds(8 * half, 8)
        sem = sending(sib_out.at[layer, k, at])
        remote(sib_out.at[layer, k, at], sib_in.at[layer, k, at], sem, sib_sem.at[layer, k, half], sibling).start()

    def shared(layer, k, half):
        arrived(sib_in.at[layer, k, pl.ds(8 * half, 8)], sib_sem.at[layer, k, half])

    def scatter(k):
        sem = sending(sums_in.at[k, pl.ds(1, NQ - 1)])
        for j in range(8):
            if j % 4 == 0:
                shared(0, k, j // 4)
            for dyh in (1, 0):
                d = 2 * Z_STEPS[j] + dyh
                if d == 0:
                    continue
                at = 2 * j + lax.rem(yh + dyh, 2)
                sums[k, d] = (own[0, k, at] + sib_in[0, k, at].astype(F32)).astype(BF)
                remote(sums.at[k, d], sums_in.at[k, d], sem, rsy_sem.at[k], to_chip(chip_at(d))).start()

    def scatter_rows(layer, k):
        for n in range(4):
            if n % 2 == 0:
                shared(layer, k, n // 2)
            blocks = []
            for m in range(4):
                at = 2 * BLOCK_PAIRS.index((4 * m + n) // 2) + n % 2
                blocks.append(own[layer, k, at] + sib_in[layer, k, at].astype(F32))
            for g in range(4):
                turned = turn([b[8 * g : 8 * g + 8] for b in blocks])
                for a in range(4):
                    last[layer - 1, k, 4 * g + a, :, n * 128 : n * 128 + 128] = turned[a].astype(BF)
        if layer == 1:
            sem = sending(z_in.at[k, pl.ds(1, 7)])
            for dz in Z_STEPS[:7]:
                zt = lax.rem(z + dz, 8)
                piece = last.at[0, k, pl.ds(2 * zt, 2)]
                remote(piece, z_in.at[k, dz], sem, z_sem.at[k], to_chip(2 * zt + yh)).start()
            return
        sem = sending(last_in.at[k, pl.ds(1, NQ - 1)])
        for d in CHIP_STEPS:
            q = chip_at(d)
            remote(last.at[1, k, q], last_in.at[k, d], sem, last_sem.at[k], to_chip(q)).start()

    def join_pairs(k):
        arrived(z_in.at[k, pl.ds(1, 7)], z_sem.at[k])
        for mine in range(2):
            at = yh if mine else 1 - yh
            total = last[0, k, 2 * z + at].astype(F32)
            for dz in range(1, 8):
                total = total + z_in[k, dz, at].astype(F32)
            if mine:
                joined[k] = total
            else:
                pair_out[k] = total.astype(BF)
                partner = to_chip(2 * z + 1 - yh)
                remote(pair_out.at[k], pair_in.at[k], sending(pair_out.at[k]), pair_sem.at[k], partner).start()

    quarter = lax.rem(chip, 4)

    def own_rows(block):
        turned = turn([block[:, m * 512 : m * 512 + 512] for m in range(4)])
        rows = jnp.where(quarter == 0, turned[0], turned[1])
        rows = jnp.where(quarter == 2, turned[2], rows)
        return jnp.where(quarter == 3, turned[3], rows)

    def add_sums(layer, k, rows):
        if layer == 1:
            arrived(pair_in.at[k], pair_sem.at[k])
            total = joined[k] + pair_in[k].astype(F32)
        else:
            arrived(last_in.at[k, pl.ds(1, NQ - 1)], last_sem.at[k])
            total = last[1, k, chip].astype(F32)
            for d in range(1, NQ):
                total = total + last_in[k, d].astype(F32)
        return (rows + total).astype(BF).astype(F32)

    def write_rows(out, pair0, pair1):
        even, odd = swap(pair0, pair1, 2)
        out[:, 0:512] = even[0:4].astype(BF)
        out[:, 512:1024] = odd[0:4].astype(BF)
        out[:, 1024:1536] = even[4:8].astype(BF)
        out[:, 1536:2048] = odd[4:8].astype(BF)

    def new_state(k):
        arrived(sums_in.at[k, pl.ds(1, NQ - 1)], rsy_sem.at[k])
        total = own[0, k, 14 + yh] + sib_in[0, k, 14 + yh].astype(F32)
        for d in range(1, NQ):
            total = total + sums_in[k, d].astype(F32)
        return (x[0, k, core, chip].astype(F32) + total).astype(BF).astype(F32)

    second_fwd = []

    def take_tokens():
        for d in CHIP_STEPS:
            arrived(tok_in.at[chip_from(d)], tok_sem.at[d])
        pair = lax.broadcasted_iota(jnp.int32, (8, 128), 0) // 2
        for k in range(CHUNKS):
            for g in range(4):
                group = jnp.zeros((8, 128), F32)
                for a in range(4):
                    t = tok_in[4 * g + a].astype(F32)
                    group = jnp.where(pair == a, t if a % 2 == k else pltpu.roll(t, 2, 0), group)
                tokens[k, 8 * g : 8 * g + 8] = group

    def spread(k):
        x[1, k, core, chip] = (new_state(k) + tokens[k]).astype(BF)
        piece = x.at[1, k, core, chip]
        sem = sending(x.at[1, k, 0, pl.ds(0, NQ - 1)])
        second_fwd.append(sending(x.at[1, k, 0]))
        for d in CHIP_STEPS:
            remote(piece, piece, sem, ag_sem.at[k, d], to_chip(chip_at(d))).start()
        remote(piece, piece, second_fwd[k], ag_fwd.at[k], sibling).start()

    def pass_on(k, steps):
        for d in steps:
            piece = x.at[1, k, core, chip_from(d)]
            arrived(piece, ag_sem.at[k, d])
            remote(piece, piece, second_fwd[k], ag_fwd.at[k], sibling).start()

    def pass_on_first(k, steps):
        for d in steps:
            piece = first.at[k, core, chip_from(d)]
            arrived(piece, first_sem.at[k, d])
            remote(piece, piece, forward[k], first_fwd.at[k], sibling).start()

    pass_on_first(0, NEAR_FIRST)
    for k in range(CHUNKS):
        if k == 1:
            pass_on_first(1, NEAR_FIRST)
        arrived(first.at[k, other], first_fwd.at[k])
        for h in range(2):
            for g in range(4):
                quarters = turn([first[k, h, 4 * g + a].astype(F32) for a in range(4)])
                for m in range(4):
                    rows_f[k, h, g, :, m * 512 : m * 512 + 512] = quarters[m]
            for cb in range(NQ):
                block = rows_f[k, h, :, :, cb * 128 : cb * 128 + 128]
                x[0, k, h, cb] = block.reshape(32, 128).astype(BF)
        prepare(0, k)
        if k == 0:
            pass
            loads[6].wait()
            loads[7].wait()
        up(0, k)
    for k in range(CHUNKS):
        act(0, k)
    take_tokens()
    loads[8].wait()
    for k in range(CHUNKS):
        hidden(0, k)
        down(0, k)
        scatter(k)
    for k in range(CHUNKS):
        spread(k)

    pass_on(0, NEAR_FIRST)
    for k in range(CHUNKS):
        if k == 1:
            pass_on(1, NEAR_FIRST)
        arrived(x.at[1, k, other], ag_fwd.at[k])
        prepare(1, k)
        if k == 0:
            pass
        up(1, k)
    for k in range(CHUNKS):
        act(1, k)
    kept_mixed = []
    for m in range(8):
        cb = 8 * core + m
        column = jnp.concatenate([x[1, k, h, cb] for k in range(CHUNKS) for h in range(2)], axis=0)
        kept_mixed.append(jnp.dot(picker, column, preferred_element_type=F32)[0:8])
    for k in range(CHUNKS):
        hidden(1, k)
        if k == 0:
            down(1, 0)

    def pick_hidden(n, carry):
        cols = pl.ds(pl.multiple_of(n * 128, 128), 128)
        chosen = jnp.zeros((16, 128), F32)
        for k in range(CHUNKS):
            rows = picker[:, 64 * k : 64 * k + 64]
            chosen = chosen + jnp.dot(rows, hid_mm[k, 0:64, cols], preferred_element_type=F32)
        hid_mm[1, 64:80, cols] = chosen.astype(BF)
        return carry

    lax.fori_loop(0, HID // 128, pick_hidden, 0)
    down(1, 1, True)

    arrived(kp_in, kp_sem.at[0])
    ks[...] = (kp[pl.ds(8 * core, 8)] + kp_in[...].astype(F32)).astype(BF)
    sem = sending(ks_in.at[pl.ds(1, NQ - 1)])
    for d in CHIP_STEPS:
        remote(ks, ks_in.at[d], sem, ks_sem.at[0], to_chip(chip_at(d))).start()
    arrived(ks_in.at[pl.ds(1, NQ - 1)], ks_sem.at[0])
    total = ks[...].astype(F32)
    for d in range(1, NQ):
        total = total + ks_in[d].astype(F32)
    for m in range(8):
        pick_all[8 * core + m] = (kept_mixed[m] + total[m]).astype(BF)
    half = pick_all.at[pl.ds(8 * core, 8)]
    remote(half, half, sending(half), pick_sem.at[0], sibling).start()
    arrived(half, pick_sem.at[0])

    upper = lax.broadcasted_iota(jnp.int32, (8, 128), 0) < 4
    for k in range(CHUNKS):
        for cb in range(NQ):
            cols = slice(cb * 128, cb * 128 + 128)
            chosen = pick_all[cb].astype(F32)
            chosen = jnp.concatenate(
                [jnp.where(upper, chosen[2 * g : 2 * g + 1], chosen[2 * g + 1 : 2 * g + 2]) for g in range(4)], axis=0
            )
            for h in range(2):
                at = 64 * k + 32 * h
                rows = (chosen + words[at : at + 32, cols].astype(F32)).astype(BF)
                x[2, k, h, cb] = rows
                rows_f[k, h, :, :, cols] = rows.astype(F32).reshape(4, 8, 128)
        prepare(2, k)
        up(2, k)

    for k in range(CHUNKS):
        scatter_rows(1, k)
    for k in range(CHUNKS):
        act(2, k)
    for k in range(CHUNKS):
        join_pairs(k)
    for k in range(CHUNKS):
        hidden(2, k)
        down(2, k)
        scatter_rows(2, k)

    group = chip // 4
    results = []
    for k in range(CHUNKS):
        columns = []
        for cb in range(NQ):
            rows = x[1, k, core, cb].astype(F32)
            eight = jnp.where(group == 0, rows[0:8], rows[8:16])
            eight = jnp.where(group == 2, rows[16:24], eight)
            columns.append(jnp.where(group == 3, rows[24:32], eight))
        results.append(add_sums(1, k, own_rows(jnp.concatenate(columns, axis=1))))
    write_rows(dec_out, *results)
    residuals = [own_rows(rows_f[k, core, group]) for k in range(CHUNKS)]
    for i, ref in enumerate(sent):
        remote(ref, ref, snd.at[i], snd.at[i], sibling).wait_send()
    write_rows(ev_out, *[add_sums(2, k, residuals[k]) for k in range(CHUNKS)])


def on_device(
    beam_states, step_tokens, norm_gain, w_gate, w_up, w_down, prompt_table, kept_beams, prompt_ids
):
    vmem = pl.BlockSpec(memory_space=pltpu.VMEM)
    hbm = pl.BlockSpec(memory_space=pltpu.HBM)
    V, dma = pltpu.VMEM, pltpu.SemaphoreType.DMA
    LK = (LAYERS, CHUNKS)
    scratch = [
        V((4, WIDTH), BF), V((2, 4, WIDTH), BF), V((WIDTH,), BF), pltpu.SMEM((8,), jnp.int32), V((8, 16), jnp.int32),
        V((WIDTH, HID), BF), V((WIDTH, HID), BF), V((HID, WIDTH), BF), V((256, WIDTH), BF),
        V((128, WIDTH), BF),
        V((CHUNKS, 2, NQ, 8, 512), BF),
        V((*LK, 2, NQ, 32, 128), BF),
        V((64, WIDTH), BF),
        V((*LK, 8, 16, 1024), BF), V((*LK, 8, 16, 1024), BF),
        V((*LK, 8, 8, HID), BF), V((CHUNKS, 80, HID), BF),
        V((*LK, NQ, 32, 128), F32),
        V((*LK, NQ, 32, 128), BF), V((*LK, NQ, 32, 128), BF),
        V((CHUNKS, NQ, 32, 128), BF), V((CHUNKS, NQ, 32, 128), BF),
        V((NQ, 8, 128), BF), V((NQ, 8, 128), BF),
        V((NQ, 8, 128), F32), V((8, 8, 128), BF), V((8, 8, 128), BF),
        V((8, 8, 128), BF), V((NQ, 8, 8, 128), BF), V((NQ, 8, 128), BF),
        V((CHUNKS, 2, 4, 8, WIDTH), F32),
        V((CHUNKS, 32, 128), F32),
        V((2, CHUNKS, NQ, 8, 512), BF), V((CHUNKS, NQ, 8, 512), BF),
        V((CHUNKS, 8, 2, 8, 512), BF), V((CHUNKS, 8, 512), F32),
        V((CHUNKS, 8, 512), BF), V((CHUNKS, 8, 512), BF),
        dma((9,)), dma((48,)), dma((CHUNKS, NQ)), dma((CHUNKS,)), dma((NQ,)),
        dma((CHUNKS, NQ)), dma((CHUNKS,)), dma(LK), dma((*LK, 8)),
        dma((*LK, 2)), dma((CHUNKS,)), dma((1,)), dma((1,)), dma((1,)), dma((CHUNKS,)), dma((CHUNKS,)), dma((CHUNKS,)),
    ]
    return pl.pallas_call(
        kernel,
        out_shape=(jax.ShapeDtypeStruct((4, WIDTH), BF), jax.ShapeDtypeStruct((4, WIDTH), BF)),
        in_specs=[hbm] * 9,
        out_specs=(vmem, vmem),
        scratch_shapes=scratch,
        compiler_params=pltpu.CompilerParams(
            collective_id=0, has_side_effects=True, vmem_limit_bytes=56 * 2**20
        ),
        name="beam_steps",
    )(
        beam_states, step_tokens, norm_gain, kept_beams, prompt_ids,
        w_gate, w_up, w_down, prompt_table,
    )


def solution(mesh):
    return jax.shard_map(
        on_device,
        mesh=mesh,
        in_specs=(
            P("gy", "gx"),
            P(None, "gy", "gx"),
            P("gx"),
            P("gx", "gy"),
            P("gx", "gy"),
            P("gy", "gx"),
            P(None, "gx"),
            P(),
            P(),
        ),
        out_specs=(P("gy", "gx"), P("gy", "gx")),
        check_vma=False,
    )
```

```python
import jax
import jax.numpy as jnp
from jax import lax
from jax.experimental import pallas as pl
from jax.experimental.pallas import tpu as pltpu
from jax.sharding import PartitionSpec as P

D = 16384
EPS = 1e-05
BF, F32 = jnp.bfloat16, jnp.float32
NX, NY = 4, 2
NQ = 16
WIDTH = 2048
HID = 896
LAYERS, CHUNKS = 3, 2
MESH = pl.DeviceIdType.MESH

CHIP_STEPS = sorted(range(1, NQ), key=lambda d: -(min(d // 2, 8 - d // 2) + 2 * (d % 2)))
Z_STEPS = (4, 3, 5, 2, 6, 1, 7, 0)
BLOCK_PAIRS = (0, 2, 4, 6, 1, 3, 5, 7)
GX_STEPS = sorted(range(1, 8), key=lambda e: (-min(e % 4, 4 - e % 4), -(e // 4)))
NEAR_FIRST = CHIP_STEPS[::-1]


def swap(a, b, rows):
    first = lax.rem(lax.broadcasted_iota(jnp.int32, a.shape, 0), 2 * rows) < rows
    return jnp.where(first, a, pltpu.roll(b, rows, 0)), jnp.where(first, pltpu.roll(a, 8 - rows, 0), b)


def turn(a):
    a0, a2 = swap(a[0], a[2], 4)
    a1, a3 = swap(a[1], a[3], 4)
    return (*swap(a0, a1, 2), *swap(a2, a3, 2))


def kernel(
    beam_hbm, tok_hbm, gain_hbm, kept_hbm, ids_hbm, wg_hbm, wu_hbm, wd_hbm, tab_hbm,
    out,
    beam, tok, gain, kept, ids, wg, wu, wd, tab, words, first, x, xs, xs_all, part, part_in, hid, hid_mm,
    own, sib_out, sib_in, sums, sums_in, tok_out, tok_in,
    kp, kp_out, kp_in, ks, ks_in, pick_all, rows_f, tokens, last, last_in, z_in, joined, pair_out, pair_in,
    load_sem, snd, first_sem, first_fwd, tok_sem, ag_sem, ag_fwd, rsx_sem, agx_sem,
    sib_sem, rsy_sem, kp_sem, ks_sem, pick_sem, last_sem, z_sem, pair_sem,
):
    gx, gy = lax.axis_index("gx"), lax.axis_index("gy")
    px, pyl = lax.rem(gx, NX), gx // NX
    core, chip = lax.rem(gy, 2), gy // 2
    yh, z = lax.rem(chip, 2), chip // 2
    other = 1 - core
    sibling = (gx, chip * 2 + other)

    def chip_at(d):
        return lax.rem(z + d // 2, 8) * 2 + lax.rem(yh + d % 2, 2)

    def chip_from(d):
        return lax.rem(z + 8 - d // 2, 8) * 2 + lax.rem(yh + d % 2, 2)

    def gx_at(e):
        return lax.rem(pyl + e // 4, NY) * NX + lax.rem(px + e % 4, NX)

    def gx_from(e):
        return lax.rem(pyl + e // 4, NY) * NX + lax.rem(px + 4 - e % 4, NX)

    def to_chip(q):
        return (gx, q * 2 + core)

    def to_gx(p):
        return (p, gy)

    def remote(src, dst, send, recv, device):
        return pltpu.make_async_remote_copy(
            src_ref=src, dst_ref=dst, send_sem=send, recv_sem=recv, device_id=device, device_id_type=MESH
        )

    def arrived(ref, recv):
        remote(ref, ref, snd.at[0], recv, sibling).wait_recv()

    sent = []

    def sending(ref):
        sent.append(ref)
        return snd.at[len(sent) - 1]

    pairs = [
        (beam_hbm, beam), (tok_hbm, tok), (tab_hbm, tab), (ids_hbm, ids), (kept_hbm, kept), (gain_hbm, gain),
        (wg_hbm, wg), (wu_hbm, wu), (wd_hbm, wd),
    ]
    loads = [pltpu.make_async_copy(s, d, load_sem.at[i]) for i, (s, d) in enumerate(pairs)]
    for load in loads:
        load.start()

    barrier = pltpu.get_barrier_semaphore()
    for d in CHIP_STEPS:
        pl.semaphore_signal(barrier, inc=1, device_id=to_chip(chip_at(d)), device_id_type=MESH)
    for e in GX_STEPS:
        pl.semaphore_signal(barrier, inc=1, device_id=to_gx(gx_at(e)), device_id_type=MESH)
    pl.semaphore_signal(barrier, inc=1, device_id=sibling, device_id_type=MESH)

    loads[0].wait()
    loads[1].wait()
    mixed = (beam[...].astype(F32) + tok[0].astype(F32)).astype(BF).astype(F32)
    mixed = jnp.concatenate([mixed, mixed], axis=0)
    top = lax.broadcasted_iota(jnp.int32, (8, 512), 0) < 4
    even, odd = swap(
        jnp.where(top, mixed[:, 0:512], mixed[:, 1024:1536]), jnp.where(top, mixed[:, 512:1024], mixed[:, 1536:2048]), 2
    )
    first[0, core, chip] = even.astype(BF)
    first[1, core, chip] = odd.astype(BF)
    token = tok[1].astype(F32)
    token = jnp.concatenate([token, token], axis=0).astype(BF)
    for cb in range(NQ):
        tok_out[cb] = token[:, cb * 128 : cb * 128 + 128]

    pl.semaphore_wait(barrier, NQ - 1 + 7 + 1)

    forward = []
    for k in range(CHUNKS):
        piece = first.at[k, core, chip]
        sem = sending(first.at[k, 0, pl.ds(0, NQ - 1)])
        forward.append(sending(first.at[k, 0]))
        for d in CHIP_STEPS:
            remote(piece, piece, sem, first_sem.at[k, d], to_chip(chip_at(d))).start()
        remote(piece, piece, forward[k], first_fwd.at[k], sibling).start()
    sem = sending(tok_in.at[pl.ds(0, NQ - 1)])
    for d in CHIP_STEPS:
        remote(tok_out.at[chip_at(d)], tok_in.at[chip], sem, tok_sem.at[d], to_chip(chip_at(d))).start()
    tok_in[chip] = tok_out[chip]

    for load in loads[2:6]:
        load.wait()

    def row_of(shape, dim):
        t = lax.broadcasted_iota(jnp.int32, shape, dim)
        return 8 * (lax.rem(t, 32) // 2) + 4 * (lax.rem(t, 64) // 32) + 2 * (t // 64) + lax.rem(t, 2)

    of_beam = (row_of((128, 8), 0) // 16 == lax.broadcasted_iota(jnp.int32, (128, 8), 1)).astype(F32).astype(BF)
    beam_ids = jnp.dot(of_beam, ids[...].astype(F32).astype(BF), preferred_element_type=F32)
    place = lax.rem(row_of((128, 16), 0), 16) == lax.broadcasted_iota(jnp.int32, (128, 16), 1)
    row_ids = jnp.sum(jnp.where(place, beam_ids, 0.0), axis=1, keepdims=True)
    lookup = (row_ids == lax.broadcasted_iota(jnp.int32, (128, 256), 1).astype(F32)).astype(F32).astype(BF)
    for n in range(4):
        cols = slice(n * 512, n * 512 + 512)
        words[:, cols] = jnp.dot(lookup, tab[:, cols], preferred_element_type=F32).astype(BF)
    nth = lax.broadcasted_iota(jnp.int32, (16, 128), 0)
    kept_rows = jnp.full((16, 128), -1, jnp.int32)
    for n in range(8):
        kept_rows = jnp.where(nth == n, kept[n], kept_rows)
    picker = (kept_rows == row_of((16, 128), 1)).astype(F32).astype(BF)

    def prepare(layer, k):
        totals = []
        for h in range(2):
            total = jnp.zeros((32, 128), F32)
            for cb in range(NQ):
                v = x[layer, k, h, cb].astype(F32)
                total = total + v * v
                cols = slice(cb * 128, cb * 128 + 128)
                xs[h * 32 : h * 32 + 32, cols] = (v * gain[cols].astype(F32)[None, :]).astype(BF)
            totals.append(total)
        put_squares(layer, k, totals)

    def put_squares(layer, k, totals):
        squares = [jnp.sum(total, axis=1, keepdims=True) for total in totals]
        whole = jnp.broadcast_to(jnp.concatenate(squares, axis=0), (64, 128))
        high = whole.astype(BF).astype(F32)
        both = jnp.concatenate([high.reshape(8, 8, 128), (whole - high).reshape(8, 8, 128)], axis=1)
        part[layer, k, :, :, HID:1024] = both.astype(BF)

    def up(layer, k):
        for n in range(HID // 128):
            cols = slice(n * 128, n * 128 + 128)
            weights = jnp.concatenate([wg[:, cols], wu[:, cols]], axis=1)
            y = jnp.dot(xs[...], weights, preferred_element_type=F32)
            both = jnp.concatenate([y[:, :128].reshape(8, 8, 128), y[:, 128:].reshape(8, 8, 128)], axis=1)
            part[layer, k, :, :, cols] = both.astype(BF)
        send_parts(layer, k)

    def send_parts(layer, k):
        sem = sending(part_in.at[layer, k, pl.ds(1, 7)])
        for e in GX_STEPS:
            p = gx_at(e)
            remote(part.at[layer, k, p], part_in.at[layer, k, e], sem, rsx_sem.at[layer, k], to_gx(p)).start()

    def act(layer, k):
        arrived(part_in.at[layer, k, pl.ds(1, 7)], rsx_sem.at[layer, k])
        total = part[layer, k, gx].astype(F32)
        for e in range(1, 8):
            total = total + part_in[layer, k, e].astype(F32)
        squares = total[0:8, HID:1024] + total[8:16, HID:1024]
        scale = lax.rsqrt(squares / D + EPS)
        for n in range(HID // 128):
            cols = slice(n * 128, n * 128 + 128)
            g = scale * total[0:8, cols]
            u = scale * total[8:16, cols]
            hid[layer, k, gx, :, cols] = (g / (1.0 + jnp.exp(-g)) * u).astype(BF)
        piece = hid.at[layer, k, gx]
        sem = sending(hid.at[layer, k, pl.ds(0, 7)])
        for e in GX_STEPS:
            remote(piece, piece, sem, agx_sem.at[layer, k, e], to_gx(gx_at(e))).start()

    def hidden(layer, k):
        for e in reversed(GX_STEPS):
            arrived(hid.at[layer, k, gx_from(e)], agx_sem.at[layer, k, e])
        hid_mm[k, 0:64] = hid[layer, k].astype(F32).reshape(64, HID).astype(BF)

    def down(layer, k, with_kept=False):
        for j in range(8):
            pair = lax.rem(z + Z_STEPS[j], 8) if layer == 0 else BLOCK_PAIRS[j]
            rows = hid_mm[k] if with_kept else hid_mm[k, 0:64]
            cols = pl.ds(pl.multiple_of(pair * 256, 256), 256) if layer == 0 else slice(pair * 256, pair * 256 + 256)
            y = jnp.dot(rows, wd[:, cols], preferred_element_type=F32)
            mine = jnp.where(core == 0, y[0:32], y[32:64])
            theirs = jnp.where(core == 0, y[32:64], y[0:32]).astype(BF)
            for m in range(2):
                own[layer, k, 2 * j + m] = mine[:, m * 128 : m * 128 + 128]
                sib_out[layer, k, 2 * j + m] = theirs[:, m * 128 : m * 128 + 128]
                if with_kept:
                    kp[2 * pair + m] = y[64:72, m * 128 : m * 128 + 128]
            if j % 4 == 3 and not with_kept:
                share_sums(layer, k, j // 4)
        if with_kept:
            kp_out[...] = kp[pl.ds(8 * other, 8)].astype(BF)
            remote(kp_out, kp_in, sending(kp_out), kp_sem.at[0], sibling).start()
            for half in range(2):
                share_sums(layer, k, half)

    def share_sums(layer, k, half):
        at = pl.ds(8 * half, 8)
        sem = sending(sib_out.at[layer, k, at])
        remote(sib_out.at[layer, k, at], sib_in.at[layer, k, at], sem, sib_sem.at[layer, k, half], sibling).start()

    def shared(layer, k, half):
        arrived(sib_in.at[layer, k, pl.ds(8 * half, 8)], sib_sem.at[layer, k, half])

    def scatter(k):
        sem = sending(sums_in.at[k, pl.ds(1, NQ - 1)])
        for j in range(8):
            if j % 4 == 0:
                shared(0, k, j // 4)
            for dyh in (1, 0):
                d = 2 * Z_STEPS[j] + dyh
                if d == 0:
                    continue
                at = 2 * j + lax.rem(yh + dyh, 2)
                sums[k, d] = (own[0, k, at] + sib_in[0, k, at].astype(F32)).astype(BF)
                remote(sums.at[k, d], sums_in.at[k, d], sem, rsy_sem.at[k], to_chip(chip_at(d))).start()

    def scatter_rows(layer, k):
        for n in range(4):
            if n % 2 == 0:
                shared(layer, k, n // 2)
            blocks = []
            for m in range(4):
                at = 2 * BLOCK_PAIRS.index((4 * m + n) // 2) + n % 2
                blocks.append(own[layer, k, at] + sib_in[layer, k, at].astype(F32))
            for g in range(4):
                turned = turn([b[8 * g : 8 * g + 8] for b in blocks])
                for a in range(4):
                    last[layer - 1, k, 4 * g + a, :, n * 128 : n * 128 + 128] = turned[a].astype(BF)
        if layer == 1:
            sem = sending(z_in.at[k, pl.ds(1, 7)])
            for dz in Z_STEPS[:7]:
                zt = lax.rem(z + dz, 8)
                piece = last.at[0, k, pl.ds(2 * zt, 2)]
                remote(piece, z_in.at[k, dz], sem, z_sem.at[k], to_chip(2 * zt + yh)).start()
            return
        sem = sending(last_in.at[k, pl.ds(1, NQ - 1)])
        for d in CHIP_STEPS:
            q = chip_at(d)
            remote(last.at[1, k, q], last_in.at[k, d], sem, last_sem.at[k], to_chip(q)).start()

    def join_pairs(k):
        arrived(z_in.at[k, pl.ds(1, 7)], z_sem.at[k])
        for mine in range(2):
            at = yh if mine else 1 - yh
            total = last[0, k, 2 * z + at].astype(F32)
            for dz in range(1, 8):
                total = total + z_in[k, dz, at].astype(F32)
            if mine:
                joined[k] = total
            else:
                pair_out[k] = total.astype(BF)
                partner = to_chip(2 * z + 1 - yh)
                remote(pair_out.at[k], pair_in.at[k], sending(pair_out.at[k]), pair_sem.at[k], partner).start()

    quarter = lax.rem(chip, 4)

    def own_rows(block):
        turned = turn([block[:, m * 512 : m * 512 + 512] for m in range(4)])
        rows = jnp.where(quarter == 0, turned[0], turned[1])
        rows = jnp.where(quarter == 2, turned[2], rows)
        return jnp.where(quarter == 3, turned[3], rows)

    def add_sums(layer, k, rows):
        if layer == 1:
            arrived(pair_in.at[k], pair_sem.at[k])
            total = joined[k] + pair_in[k].astype(F32)
        else:
            arrived(last_in.at[k, pl.ds(1, NQ - 1)], last_sem.at[k])
            total = last[1, k, chip].astype(F32)
            for d in range(1, NQ):
                total = total + last_in[k, d].astype(F32)
        return (rows + total).astype(BF).astype(F32)

    def write_rows(out, pair0, pair1):
        even, odd = swap(pair0, pair1, 2)
        out[:, 0:512] = even[0:4].astype(BF)
        out[:, 512:1024] = odd[0:4].astype(BF)
        out[:, 1024:1536] = even[4:8].astype(BF)
        out[:, 1536:2048] = odd[4:8].astype(BF)

    def new_state(k):
        arrived(sums_in.at[k, pl.ds(1, NQ - 1)], rsy_sem.at[k])
        total = own[0, k, 14 + yh] + sib_in[0, k, 14 + yh].astype(F32)
        for d in range(1, NQ):
            total = total + sums_in[k, d].astype(F32)
        return (x[0, k, core, chip].astype(F32) + total).astype(BF).astype(F32)

    second_fwd = []

    def take_tokens():
        for d in CHIP_STEPS:
            arrived(tok_in.at[chip_from(d)], tok_sem.at[d])
        pair = lax.broadcasted_iota(jnp.int32, (8, 128), 0) // 2
        for k in range(CHUNKS):
            for g in range(4):
                group = jnp.zeros((8, 128), F32)
                for a in range(4):
                    t = tok_in[4 * g + a].astype(F32)
                    group = jnp.where(pair == a, t if a % 2 == k else pltpu.roll(t, 2, 0), group)
                tokens[k, 8 * g : 8 * g + 8] = group

    def spread(k):
        x[1, k, core, chip] = (new_state(k) + tokens[k]).astype(BF)
        piece = x.at[1, k, core, chip]
        sem = sending(x.at[1, k, 0, pl.ds(0, NQ - 1)])
        second_fwd.append(sending(x.at[1, k, 0]))
        for d in CHIP_STEPS:
            remote(piece, piece, sem, ag_sem.at[k, d], to_chip(chip_at(d))).start()
        remote(piece, piece, second_fwd[k], ag_fwd.at[k], sibling).start()

    def pass_on(k, steps):
        for d in steps:
            piece = x.at[1, k, core, chip_from(d)]
            arrived(piece, ag_sem.at[k, d])
            remote(piece, piece, second_fwd[k], ag_fwd.at[k], sibling).start()

    def pass_on_first(k, steps):
        for d in steps:
            piece = first.at[k, core, chip_from(d)]
            arrived(piece, first_sem.at[k, d])
            remote(piece, piece, forward[k], first_fwd.at[k], sibling).start()

    pass_on_first(0, NEAR_FIRST)
    for k in range(CHUNKS):
        if k == 1:
            pass_on_first(1, NEAR_FIRST)
        arrived(first.at[k, other], first_fwd.at[k])
        for h in range(2):
            for g in range(4):
                quarters = turn([first[k, h, 4 * g + a].astype(F32) for a in range(4)])
                for m in range(4):
                    rows_f[k, h, g, :, m * 512 : m * 512 + 512] = quarters[m]
            for cb in range(NQ):
                block = rows_f[k, h, :, :, cb * 128 : cb * 128 + 128]
                x[0, k, h, cb] = block.reshape(32, 128).astype(BF)
        prepare(0, k)
        if k == 0:
            pass
            loads[6].wait()
            loads[7].wait()
        up(0, k)
    for k in range(CHUNKS):
        act(0, k)
    take_tokens()
    loads[8].wait()
    for k in range(CHUNKS):
        hidden(0, k)
        down(0, k)
        scatter(k)
    for k in range(CHUNKS):
        spread(k)

    pass_on(0, NEAR_FIRST)
    for k in range(CHUNKS):
        if k == 1:
            pass_on(1, NEAR_FIRST)
        arrived(x.at[1, k, other], ag_fwd.at[k])
        prepare(1, k)
        if k == 0:
            pass
        up(1, k)
    for k in range(CHUNKS):
        act(1, k)
    kept_mixed = []
    for m in range(8):
        cb = 8 * core + m
        column = jnp.concatenate([x[1, k, h, cb] for k in range(CHUNKS) for h in range(2)], axis=0)
        kept_mixed.append(jnp.dot(picker, column, preferred_element_type=F32)[0:8])
    for k in range(CHUNKS):
        hidden(1, k)
        if k == 0:
            down(1, 0)

    def pick_hidden(n, carry):
        cols = pl.ds(pl.multiple_of(n * 128, 128), 128)
        chosen = jnp.zeros((16, 128), F32)
        for k in range(CHUNKS):
            rows = picker[:, 64 * k : 64 * k + 64]
            chosen = chosen + jnp.dot(rows, hid_mm[k, 0:64, cols], preferred_element_type=F32)
        hid_mm[1, 64:80, cols] = chosen.astype(BF)
        return carry

    lax.fori_loop(0, HID // 128, pick_hidden, 0)
    down(1, 1, True)

    arrived(kp_in, kp_sem.at[0])
    ks[...] = (kp[pl.ds(8 * core, 8)] + kp_in[...].astype(F32)).astype(BF)
    sem = sending(ks_in.at[pl.ds(1, NQ - 1)])
    for d in CHIP_STEPS:
        remote(ks, ks_in.at[d], sem, ks_sem.at[0], to_chip(chip_at(d))).start()
    arrived(ks_in.at[pl.ds(1, NQ - 1)], ks_sem.at[0])
    total = ks[...].astype(F32)
    for d in range(1, NQ):
        total = total + ks_in[d].astype(F32)
    for m in range(8):
        pick_all[8 * core + m] = (kept_mixed[m] + total[m]).astype(BF)
    half = pick_all.at[pl.ds(8 * core, 8)]
    remote(half, half, sending(half), pick_sem.at[0], sibling).start()
    arrived(half, pick_sem.at[0])

    upper = lax.broadcasted_iota(jnp.int32, (8, 128), 0) < 4
    for k in range(CHUNKS):
        totals = [jnp.zeros((32, 128), F32) for h in range(2)]
        for cb in range(NQ):
            cols = slice(cb * 128, cb * 128 + 128)
            chosen = pick_all[cb].astype(F32)
            chosen = jnp.concatenate(
                [jnp.where(upper, chosen[2 * g : 2 * g + 1], chosen[2 * g + 1 : 2 * g + 2]) for g in range(4)], axis=0
            )
            for h in range(2):
                at = 64 * k + 32 * h
                rows = (chosen + words[at : at + 32, cols].astype(F32)).astype(BF).astype(F32)
                rows_f[k, h, :, :, cols] = rows.reshape(4, 8, 128)
                totals[h] = totals[h] + rows * rows
                xs_all[at : at + 32, cols] = (rows * gain[cols].astype(F32)[None, :]).astype(BF)
        put_squares(2, k, totals)
    for n in range(HID // 128):
        cols = slice(n * 128, n * 128 + 128)
        weights = jnp.concatenate([wg[:, cols], wu[:, cols]], axis=1)
        y = jnp.dot(xs_all[...], weights, preferred_element_type=F32)
        for k in range(CHUNKS):
            rows = y[64 * k : 64 * k + 64]
            both = jnp.concatenate([rows[:, :128].reshape(8, 8, 128), rows[:, 128:].reshape(8, 8, 128)], axis=1)
            part[2, k, :, :, cols] = both.astype(BF)
    for k in range(CHUNKS):
        send_parts(2, k)

    for k in range(CHUNKS):
        scatter_rows(1, k)
    for k in range(CHUNKS):
        act(2, k)
    for k in range(CHUNKS):
        join_pairs(k)
    for k in range(CHUNKS):
        hidden(2, k)
        down(2, k)
        scatter_rows(2, k)

    group = chip // 4
    results = []
    for k in range(CHUNKS):
        columns = []
        for cb in range(NQ):
            rows = x[1, k, core, cb].astype(F32)
            eight = jnp.where(group == 0, rows[0:8], rows[8:16])
            eight = jnp.where(group == 2, rows[16:24], eight)
            columns.append(jnp.where(group == 3, rows[24:32], eight))
        results.append(add_sums(1, k, own_rows(jnp.concatenate(columns, axis=1))))
    write_rows(out.at[0], *results)
    residuals = [own_rows(rows_f[k, core, group]) for k in range(CHUNKS)]
    for i, ref in enumerate(sent):
        remote(ref, ref, snd.at[i], snd.at[i], sibling).wait_send()
    write_rows(out.at[1], *[add_sums(2, k, residuals[k]) for k in range(CHUNKS)])


def on_device(
    beam_states, step_tokens, norm_gain, w_gate, w_up, w_down, prompt_table, kept_beams, prompt_ids
):
    vmem = pl.BlockSpec(memory_space=pltpu.VMEM)
    hbm = pl.BlockSpec(memory_space=pltpu.HBM)
    V, dma = pltpu.VMEM, pltpu.SemaphoreType.DMA
    LK = (LAYERS, CHUNKS)
    scratch = [
        V((4, WIDTH), BF), V((2, 4, WIDTH), BF), V((WIDTH,), BF), pltpu.SMEM((8,), jnp.int32), V((8, 16), jnp.int32),
        V((WIDTH, HID), BF), V((WIDTH, HID), BF), V((HID, WIDTH), BF), V((256, WIDTH), BF),
        V((128, WIDTH), BF),
        V((CHUNKS, 2, NQ, 8, 512), BF),
        V((2, CHUNKS, 2, NQ, 32, 128), BF),
        V((64, WIDTH), BF), V((128, WIDTH), BF),
        V((*LK, 8, 16, 1024), BF), V((*LK, 8, 16, 1024), BF),
        V((*LK, 8, 8, HID), BF), V((CHUNKS, 80, HID), BF),
        V((*LK, NQ, 32, 128), F32),
        V((*LK, NQ, 32, 128), BF), V((*LK, NQ, 32, 128), BF),
        V((CHUNKS, NQ, 32, 128), BF), V((CHUNKS, NQ, 32, 128), BF),
        V((NQ, 8, 128), BF), V((NQ, 8, 128), BF),
        V((NQ, 8, 128), F32), V((8, 8, 128), BF), V((8, 8, 128), BF),
        V((8, 8, 128), BF), V((NQ, 8, 8, 128), BF), V((NQ, 8, 128), BF),
        V((CHUNKS, 2, 4, 8, WIDTH), F32),
        V((CHUNKS, 32, 128), F32),
        V((2, CHUNKS, NQ, 8, 512), BF), V((CHUNKS, NQ, 8, 512), BF),
        V((CHUNKS, 8, 2, 8, 512), BF), V((CHUNKS, 8, 512), F32),
        V((CHUNKS, 8, 512), BF), V((CHUNKS, 8, 512), BF),
        dma((9,)), dma((48,)), dma((CHUNKS, NQ)), dma((CHUNKS,)), dma((NQ,)),
        dma((CHUNKS, NQ)), dma((CHUNKS,)), dma(LK), dma((*LK, 8)),
        dma((*LK, 2)), dma((CHUNKS,)), dma((1,)), dma((1,)), dma((1,)), dma((CHUNKS,)), dma((CHUNKS,)), dma((CHUNKS,)),
    ]
    both = pl.pallas_call(
        kernel,
        out_shape=jax.ShapeDtypeStruct((2, 4, WIDTH), BF),
        in_specs=[hbm] * 9,
        out_specs=vmem,
        scratch_shapes=scratch,
        compiler_params=pltpu.CompilerParams(
            collective_id=0, has_side_effects=True, vmem_limit_bytes=56 * 2**20
        ),
        name="beam_steps",
    )(
        beam_states, step_tokens, norm_gain, kept_beams, prompt_ids,
        w_gate, w_up, w_down, prompt_table,
    )
    return both[0], both[1]


def solution(mesh):
    return jax.shard_map(
        on_device,
        mesh=mesh,
        in_specs=(
            P("gy", "gx"),
            P(None, "gy", "gx"),
            P("gx"),
            P("gx", "gy"),
            P("gx", "gy"),
            P("gy", "gx"),
            P(None, "gx"),
            P(),
            P(),
        ),
        out_specs=(P("gy", "gx"), P("gy", "gx")),
        check_vma=False,
    )
```

```python
import jax
import jax.numpy as jnp
from jax import lax
from jax.experimental import pallas as pl
from jax.experimental.pallas import tpu as pltpu
from jax.sharding import PartitionSpec as P

D = 16384
EPS = 1e-05
BF, F32 = jnp.bfloat16, jnp.float32
NX, NY = 4, 2
NQ = 16
WIDTH = 2048
HID = 896
LAYERS, CHUNKS = 3, 2
MESH = pl.DeviceIdType.MESH

CHIP_STEPS = sorted(range(1, NQ), key=lambda d: (-(d % 2), -min(d // 2, 8 - d // 2)))
Z_STEPS = (4, 3, 5, 2, 6, 1, 7, 0)
BLOCK_PAIRS = (0, 2, 4, 6, 1, 3, 5, 7)
GX_STEPS = sorted(range(1, 8), key=lambda e: (-min(e % 4, 4 - e % 4), -(e // 4)))
NEAR_FIRST = CHIP_STEPS[::-1]


def swap(a, b, rows):
    first = lax.rem(lax.broadcasted_iota(jnp.int32, a.shape, 0), 2 * rows) < rows
    return jnp.where(first, a, pltpu.roll(b, rows, 0)), jnp.where(first, pltpu.roll(a, 8 - rows, 0), b)


def turn(a):
    a0, a2 = swap(a[0], a[2], 4)
    a1, a3 = swap(a[1], a[3], 4)
    return (*swap(a0, a1, 2), *swap(a2, a3, 2))


def kernel(
    beam_hbm, tok_hbm, gain_hbm, kept_hbm, ids_hbm, wg_hbm, wu_hbm, wd_hbm, tab_hbm,
    out,
    beam, tok, gain, kept, ids, wg, wu, wd, tab, words, first, x, xs, xs_all, part, part_in, hid, hid_mm,
    own, sib_out, sib_in, sums, sums_in, tok_out, tok_in,
    kp, kp_out, kp_in, ks, ks_in, pick_all, rows_f, tokens, last, last_in, z_in, joined, pair_out, pair_in,
    load_sem, snd, first_sem, first_fwd, tok_sem, ag_sem, ag_fwd, rsx_sem, agx_sem,
    sib_sem, rsy_sem, kp_sem, ks_sem, pick_sem, last_sem, z_sem, pair_sem,
):
    gx, gy = lax.axis_index("gx"), lax.axis_index("gy")
    px, pyl = lax.rem(gx, NX), gx // NX
    core, chip = lax.rem(gy, 2), gy // 2
    yh, z = lax.rem(chip, 2), chip // 2
    other = 1 - core
    sibling = (gx, chip * 2 + other)

    def chip_at(d):
        return lax.rem(z + d // 2, 8) * 2 + lax.rem(yh + d % 2, 2)

    def chip_from(d):
        return lax.rem(z + 8 - d // 2, 8) * 2 + lax.rem(yh + d % 2, 2)

    def gx_at(e):
        return lax.rem(pyl + e // 4, NY) * NX + lax.rem(px + e % 4, NX)

    def gx_from(e):
        return lax.rem(pyl + e // 4, NY) * NX + lax.rem(px + 4 - e % 4, NX)

    def to_chip(q):
        return (gx, q * 2 + core)

    def to_gx(p):
        return (p, gy)

    def remote(src, dst, send, recv, device):
        return pltpu.make_async_remote_copy(
            src_ref=src, dst_ref=dst, send_sem=send, recv_sem=recv, device_id=device, device_id_type=MESH
        )

    def arrived(ref, recv):
        remote(ref, ref, snd.at[0], recv, sibling).wait_recv()

    sent = []

    def sending(ref):
        sent.append(ref)
        return snd.at[len(sent) - 1]

    pairs = [
        (beam_hbm, beam), (tok_hbm, tok), (tab_hbm, tab), (ids_hbm, ids), (kept_hbm, kept), (gain_hbm, gain),
        (wg_hbm, wg), (wu_hbm, wu), (wd_hbm, wd),
    ]
    loads = [pltpu.make_async_copy(s, d, load_sem.at[i]) for i, (s, d) in enumerate(pairs)]
    for load in loads:
        load.start()

    barrier = pltpu.get_barrier_semaphore()
    for d in CHIP_STEPS:
        pl.semaphore_signal(barrier, inc=1, device_id=to_chip(chip_at(d)), device_id_type=MESH)
    for e in GX_STEPS:
        pl.semaphore_signal(barrier, inc=1, device_id=to_gx(gx_at(e)), device_id_type=MESH)
    pl.semaphore_signal(barrier, inc=1, device_id=sibling, device_id_type=MESH)

    loads[0].wait()
    loads[1].wait()
    mixed = (beam[...].astype(F32) + tok[0].astype(F32)).astype(BF).astype(F32)
    mixed = jnp.concatenate([mixed, mixed], axis=0)
    top = lax.broadcasted_iota(jnp.int32, (8, 512), 0) < 4
    even, odd = swap(
        jnp.where(top, mixed[:, 0:512], mixed[:, 1024:1536]), jnp.where(top, mixed[:, 512:1024], mixed[:, 1536:2048]), 2
    )
    first[0, core, chip] = even.astype(BF)
    first[1, core, chip] = odd.astype(BF)
    token = tok[1].astype(F32)
    token = jnp.concatenate([token, token], axis=0).astype(BF)
    for cb in range(NQ):
        tok_out[cb] = token[:, cb * 128 : cb * 128 + 128]

    pl.semaphore_wait(barrier, NQ - 1 + 7 + 1)

    forward = []
    for k in range(CHUNKS):
        piece = first.at[k, core, chip]
        sem = sending(first.at[k, 0, pl.ds(0, NQ - 1)])
        forward.append(sending(first.at[k, 0]))
        for d in CHIP_STEPS:
            remote(piece, piece, sem, first_sem.at[k, d], to_chip(chip_at(d))).start()
        remote(piece, piece, forward[k], first_fwd.at[k], sibling).start()
    sem = sending(tok_in.at[pl.ds(0, NQ - 1)])
    for d in CHIP_STEPS:
        remote(tok_out.at[chip_at(d)], tok_in.at[chip], sem, tok_sem.at[d], to_chip(chip_at(d))).start()
    tok_in[chip] = tok_out[chip]

    for load in loads[2:6]:
        load.wait()

    def row_of(shape, dim):
        t = lax.broadcasted_iota(jnp.int32, shape, dim)
        return 8 * (lax.rem(t, 32) // 2) + 4 * (lax.rem(t, 64) // 32) + 2 * (t // 64) + lax.rem(t, 2)

    of_beam = (row_of((128, 8), 0) // 16 == lax.broadcasted_iota(jnp.int32, (128, 8), 1)).astype(F32).astype(BF)
    beam_ids = jnp.dot(of_beam, ids[...].astype(F32).astype(BF), preferred_element_type=F32)
    place = lax.rem(row_of((128, 16), 0), 16) == lax.broadcasted_iota(jnp.int32, (128, 16), 1)
    row_ids = jnp.sum(jnp.where(place, beam_ids, 0.0), axis=1, keepdims=True)
    lookup = (row_ids == lax.broadcasted_iota(jnp.int32, (128, 256), 1).astype(F32)).astype(F32).astype(BF)
    for n in range(4):
        cols = slice(n * 512, n * 512 + 512)
        words[:, cols] = jnp.dot(lookup, tab[:, cols], preferred_element_type=F32).astype(BF)
    nth = lax.broadcasted_iota(jnp.int32, (16, 128), 0)
    kept_rows = jnp.full((16, 128), -1, jnp.int32)
    for n in range(8):
        kept_rows = jnp.where(nth == n, kept[n], kept_rows)
    picker = (kept_rows == row_of((16, 128), 1)).astype(F32).astype(BF)

    def prepare(layer, k):
        totals = []
        for h in range(2):
            total = jnp.zeros((32, 128), F32)
            for cb in range(NQ):
                v = x[layer, k, h, cb].astype(F32)
                total = total + v * v
                cols = slice(cb * 128, cb * 128 + 128)
                xs[h * 32 : h * 32 + 32, cols] = (v * gain[cols].astype(F32)[None, :]).astype(BF)
            totals.append(total)
        put_squares(layer, k, totals)

    def put_squares(layer, k, totals):
        squares = [jnp.sum(total, axis=1, keepdims=True) for total in totals]
        whole = jnp.broadcast_to(jnp.concatenate(squares, axis=0), (64, 128))
        high = whole.astype(BF).astype(F32)
        both = jnp.concatenate([high.reshape(8, 8, 128), (whole - high).reshape(8, 8, 128)], axis=1)
        part[layer, k, :, :, HID:1024] = both.astype(BF)

    def up(layer, k):
        for n in range(HID // 128):
            cols = slice(n * 128, n * 128 + 128)
            weights = jnp.concatenate([wg[:, cols], wu[:, cols]], axis=1)
            y = jnp.dot(xs[...], weights, preferred_element_type=F32)
            both = jnp.concatenate([y[:, :128].reshape(8, 8, 128), y[:, 128:].reshape(8, 8, 128)], axis=1)
            part[layer, k, :, :, cols] = both.astype(BF)
        send_parts(layer, k)

    def send_parts(layer, k):
        sem = sending(part_in.at[layer, k, pl.ds(1, 7)])
        for e in GX_STEPS:
            p = gx_at(e)
            remote(part.at[layer, k, p], part_in.at[layer, k, e], sem, rsx_sem.at[layer, k], to_gx(p)).start()

    def act(layer, k):
        arrived(part_in.at[layer, k, pl.ds(1, 7)], rsx_sem.at[layer, k])
        total = part[layer, k, gx].astype(F32)
        for e in range(1, 8):
            total = total + part_in[layer, k, e].astype(F32)
        squares = total[0:8, HID:1024] + total[8:16, HID:1024]
        scale = lax.rsqrt(squares / D + EPS)
        for n in range(HID // 128):
            cols = slice(n * 128, n * 128 + 128)
            g = scale * total[0:8, cols]
            u = scale * total[8:16, cols]
            hid[layer, k, gx, :, cols] = (g / (1.0 + jnp.exp(-g)) * u).astype(BF)
        piece = hid.at[layer, k, gx]
        sem = sending(hid.at[layer, k, pl.ds(0, 7)])
        for e in GX_STEPS:
            remote(piece, piece, sem, agx_sem.at[layer, k, e], to_gx(gx_at(e))).start()

    def hidden(layer, k):
        for e in reversed(GX_STEPS):
            arrived(hid.at[layer, k, gx_from(e)], agx_sem.at[layer, k, e])
        hid_mm[k, 0:64] = hid[layer, k].astype(F32).reshape(64, HID).astype(BF)

    def down(layer, k, with_kept=False):
        for j in range(8):
            pair = lax.rem(z + Z_STEPS[j], 8) if layer == 0 else BLOCK_PAIRS[j]
            rows = hid_mm[k] if with_kept else hid_mm[k, 0:64]
            cols = pl.ds(pl.multiple_of(pair * 256, 256), 256) if layer == 0 else slice(pair * 256, pair * 256 + 256)
            y = jnp.dot(rows, wd[:, cols], preferred_element_type=F32)
            mine = jnp.where(core == 0, y[0:32], y[32:64])
            theirs = jnp.where(core == 0, y[32:64], y[0:32]).astype(BF)
            for m in range(2):
                own[layer, k, 2 * j + m] = mine[:, m * 128 : m * 128 + 128]
                sib_out[layer, k, 2 * j + m] = theirs[:, m * 128 : m * 128 + 128]
                if with_kept:
                    kp[2 * pair + m] = y[64:72, m * 128 : m * 128 + 128]
            if j % 4 == 3 and not with_kept:
                share_sums(layer, k, j // 4)
        if with_kept:
            kp_out[...] = kp[pl.ds(8 * other, 8)].astype(BF)
            remote(kp_out, kp_in, sending(kp_out), kp_sem.at[0], sibling).start()
            for half in range(2):
                share_sums(layer, k, half)

    def share_sums(layer, k, half):
        at = pl.ds(8 * half, 8)
        sem = sending(sib_out.at[layer, k, at])
        remote(sib_out.at[layer, k, at], sib_in.at[layer, k, at], sem, sib_sem.at[layer, k, half], sibling).start()

    def shared(layer, k, half):
        arrived(sib_in.at[layer, k, pl.ds(8 * half, 8)], sib_sem.at[layer, k, half])

    def scatter(k):
        sem = sending(sums_in.at[k, pl.ds(1, NQ - 1)])
        for j in range(8):
            if j % 4 == 0:
                shared(0, k, j // 4)
            for dyh in (1, 0):
                d = 2 * Z_STEPS[j] + dyh
                if d == 0:
                    continue
                at = 2 * j + lax.rem(yh + dyh, 2)
                sums[k, d] = (own[0, k, at] + sib_in[0, k, at].astype(F32)).astype(BF)
                remote(sums.at[k, d], sums_in.at[k, d], sem, rsy_sem.at[k], to_chip(chip_at(d))).start()

    def scatter_rows(layer, k):
        for n in range(4):
            if n % 2 == 0:
                shared(layer, k, n // 2)
            blocks = []
            for m in range(4):
                at = 2 * BLOCK_PAIRS.index((4 * m + n) // 2) + n % 2
                blocks.append(own[layer, k, at] + sib_in[layer, k, at].astype(F32))
            for g in range(4):
                turned = turn([b[8 * g : 8 * g + 8] for b in blocks])
                for a in range(4):
                    last[layer - 1, k, 4 * g + a, :, n * 128 : n * 128 + 128] = turned[a].astype(BF)
        if layer == 1:
            sem = sending(z_in.at[k, pl.ds(1, 7)])
            for dz in Z_STEPS[:7]:
                zt = lax.rem(z + dz, 8)
                piece = last.at[0, k, pl.ds(2 * zt, 2)]
                remote(piece, z_in.at[k, dz], sem, z_sem.at[k], to_chip(2 * zt + yh)).start()
            return
        sem = sending(last_in.at[k, pl.ds(1, NQ - 1)])
        for d in CHIP_STEPS:
            q = chip_at(d)
            remote(last.at[1, k, q], last_in.at[k, d], sem, last_sem.at[k], to_chip(q)).start()

    def join_pairs(k):
        arrived(z_in.at[k, pl.ds(1, 7)], z_sem.at[k])
        for mine in range(2):
            at = yh if mine else 1 - yh
            total = last[0, k, 2 * z + at].astype(F32)
            for dz in range(1, 8):
                total = total + z_in[k, dz, at].astype(F32)
            if mine:
                joined[k] = total
            else:
                pair_out[k] = total.astype(BF)
                partner = to_chip(2 * z + 1 - yh)
                remote(pair_out.at[k], pair_in.at[k], sending(pair_out.at[k]), pair_sem.at[k], partner).start()

    quarter = lax.rem(chip, 4)

    def own_rows(block):
        turned = turn([block[:, m * 512 : m * 512 + 512] for m in range(4)])
        rows = jnp.where(quarter == 0, turned[0], turned[1])
        rows = jnp.where(quarter == 2, turned[2], rows)
        return jnp.where(quarter == 3, turned[3], rows)

    def add_sums(layer, k, rows):
        if layer == 1:
            arrived(pair_in.at[k], pair_sem.at[k])
            total = joined[k] + pair_in[k].astype(F32)
        else:
            arrived(last_in.at[k, pl.ds(1, NQ - 1)], last_sem.at[k])
            total = last[1, k, chip].astype(F32)
            for d in range(1, NQ):
                total = total + last_in[k, d].astype(F32)
        return (rows + total).astype(BF).astype(F32)

    def write_rows(out, pair0, pair1):
        even, odd = swap(pair0, pair1, 2)
        out[:, 0:512] = even[0:4].astype(BF)
        out[:, 512:1024] = odd[0:4].astype(BF)
        out[:, 1024:1536] = even[4:8].astype(BF)
        out[:, 1536:2048] = odd[4:8].astype(BF)

    def new_state(k):
        arrived(sums_in.at[k, pl.ds(1, NQ - 1)], rsy_sem.at[k])
        total = own[0, k, 14 + yh] + sib_in[0, k, 14 + yh].astype(F32)
        for d in range(1, NQ):
            total = total + sums_in[k, d].astype(F32)
        return (x[0, k, core, chip].astype(F32) + total).astype(BF).astype(F32)

    second_fwd = []

    def take_tokens():
        for d in CHIP_STEPS:
            arrived(tok_in.at[chip_from(d)], tok_sem.at[d])
        pair = lax.broadcasted_iota(jnp.int32, (8, 128), 0) // 2
        for k in range(CHUNKS):
            for g in range(4):
                group = jnp.zeros((8, 128), F32)
                for a in range(4):
                    t = tok_in[4 * g + a].astype(F32)
                    group = jnp.where(pair == a, t if a % 2 == k else pltpu.roll(t, 2, 0), group)
                tokens[k, 8 * g : 8 * g + 8] = group

    def spread(k):
        x[1, k, core, chip] = (new_state(k) + tokens[k]).astype(BF)
        piece = x.at[1, k, core, chip]
        sem = sending(x.at[1, k, 0, pl.ds(0, NQ - 1)])
        second_fwd.append(sending(x.at[1, k, 0]))
        for d in CHIP_STEPS:
            remote(piece, piece, sem, ag_sem.at[k, d], to_chip(chip_at(d))).start()
        remote(piece, piece, second_fwd[k], ag_fwd.at[k], sibling).start()

    def pass_on(k, steps):
        for d in steps:
            piece = x.at[1, k, core, chip_from(d)]
            arrived(piece, ag_sem.at[k, d])
            remote(piece, piece, second_fwd[k], ag_fwd.at[k], sibling).start()

    def pass_on_first(k, steps):
        for d in steps:
            piece = first.at[k, core, chip_from(d)]
            arrived(piece, first_sem.at[k, d])
            remote(piece, piece, forward[k], first_fwd.at[k], sibling).start()

    pass_on_first(0, NEAR_FIRST)
    for k in range(CHUNKS):
        if k == 1:
            pass_on_first(1, NEAR_FIRST)
        arrived(first.at[k, other], first_fwd.at[k])
        for h in range(2):
            for g in range(4):
                quarters = turn([first[k, h, 4 * g + a].astype(F32) for a in range(4)])
                for m in range(4):
                    rows_f[k, h, g, :, m * 512 : m * 512 + 512] = quarters[m]
            for cb in range(NQ):
                block = rows_f[k, h, :, :, cb * 128 : cb * 128 + 128]
                x[0, k, h, cb] = block.reshape(32, 128).astype(BF)
        prepare(0, k)
        if k == 0:
            pass
            loads[6].wait()
            loads[7].wait()
        up(0, k)
    for k in range(CHUNKS):
        act(0, k)
    take_tokens()
    loads[8].wait()
    for k in range(CHUNKS):
        hidden(0, k)
        down(0, k)
        scatter(k)
    for k in range(CHUNKS):
        spread(k)

    pass_on(0, NEAR_FIRST)
    for k in range(CHUNKS):
        if k == 1:
            pass_on(1, NEAR_FIRST)
        arrived(x.at[1, k, other], ag_fwd.at[k])
        prepare(1, k)
        if k == 0:
            pass
        up(1, k)
    for k in range(CHUNKS):
        act(1, k)
    kept_mixed = []
    for m in range(8):
        cb = 8 * core + m
        column = jnp.concatenate([x[1, k, h, cb] for k in range(CHUNKS) for h in range(2)], axis=0)
        kept_mixed.append(jnp.dot(picker, column, preferred_element_type=F32)[0:8])
    for k in range(CHUNKS):
        hidden(1, k)
        if k == 0:
            down(1, 0)

    def pick_hidden(n, carry):
        cols = pl.ds(pl.multiple_of(n * 128, 128), 128)
        chosen = jnp.zeros((16, 128), F32)
        for k in range(CHUNKS):
            rows = picker[:, 64 * k : 64 * k + 64]
            chosen = chosen + jnp.dot(rows, hid_mm[k, 0:64, cols], preferred_element_type=F32)
        hid_mm[1, 64:80, cols] = chosen.astype(BF)
        return carry

    lax.fori_loop(0, HID // 128, pick_hidden, 0)
    down(1, 1, True)

    arrived(kp_in, kp_sem.at[0])
    ks[...] = (kp[pl.ds(8 * core, 8)] + kp_in[...].astype(F32)).astype(BF)
    sem = sending(ks_in.at[pl.ds(1, NQ - 1)])
    for d in CHIP_STEPS:
        remote(ks, ks_in.at[d], sem, ks_sem.at[0], to_chip(chip_at(d))).start()
    arrived(ks_in.at[pl.ds(1, NQ - 1)], ks_sem.at[0])
    total = ks[...].astype(F32)
    for d in range(1, NQ):
        total = total + ks_in[d].astype(F32)
    for m in range(8):
        pick_all[8 * core + m] = (kept_mixed[m] + total[m]).astype(BF)
    half = pick_all.at[pl.ds(8 * core, 8)]
    remote(half, half, sending(half), pick_sem.at[0], sibling).start()
    arrived(half, pick_sem.at[0])

    upper = lax.broadcasted_iota(jnp.int32, (8, 128), 0) < 4
    for k in range(CHUNKS):
        totals = [jnp.zeros((32, 128), F32) for h in range(2)]
        for cb in range(NQ):
            cols = slice(cb * 128, cb * 128 + 128)
            chosen = pick_all[cb].astype(F32)
            chosen = jnp.concatenate(
                [jnp.where(upper, chosen[2 * g : 2 * g + 1], chosen[2 * g + 1 : 2 * g + 2]) for g in range(4)], axis=0
            )
            for h in range(2):
                at = 64 * k + 32 * h
                rows = (chosen + words[at : at + 32, cols].astype(F32)).astype(BF).astype(F32)
                rows_f[k, h, :, :, cols] = rows.reshape(4, 8, 128)
                totals[h] = totals[h] + rows * rows
                xs_all[at : at + 32, cols] = (rows * gain[cols].astype(F32)[None, :]).astype(BF)
        put_squares(2, k, totals)
    for n in range(HID // 128):
        cols = slice(n * 128, n * 128 + 128)
        weights = jnp.concatenate([wg[:, cols], wu[:, cols]], axis=1)
        y = jnp.dot(xs_all[...], weights, preferred_element_type=F32)
        for k in range(CHUNKS):
            rows = y[64 * k : 64 * k + 64]
            both = jnp.concatenate([rows[:, :128].reshape(8, 8, 128), rows[:, 128:].reshape(8, 8, 128)], axis=1)
            part[2, k, :, :, cols] = both.astype(BF)
    for k in range(CHUNKS):
        send_parts(2, k)

    for k in range(CHUNKS):
        scatter_rows(1, k)
    for k in range(CHUNKS):
        act(2, k)
    for k in range(CHUNKS):
        join_pairs(k)
    for k in range(CHUNKS):
        hidden(2, k)
        down(2, k)
        scatter_rows(2, k)

    group = chip // 4
    results = []
    for k in range(CHUNKS):
        columns = []
        for cb in range(NQ):
            rows = x[1, k, core, cb].astype(F32)
            eight = jnp.where(group == 0, rows[0:8], rows[8:16])
            eight = jnp.where(group == 2, rows[16:24], eight)
            columns.append(jnp.where(group == 3, rows[24:32], eight))
        results.append(add_sums(1, k, own_rows(jnp.concatenate(columns, axis=1))))
    write_rows(out.at[0], *results)
    residuals = [own_rows(rows_f[k, core, group]) for k in range(CHUNKS)]
    for i, ref in enumerate(sent):
        remote(ref, ref, snd.at[i], snd.at[i], sibling).wait_send()
    write_rows(out.at[1], *[add_sums(2, k, residuals[k]) for k in range(CHUNKS)])


def on_device(
    beam_states, step_tokens, norm_gain, w_gate, w_up, w_down, prompt_table, kept_beams, prompt_ids
):
    vmem = pl.BlockSpec(memory_space=pltpu.VMEM)
    hbm = pl.BlockSpec(memory_space=pltpu.HBM)
    V, dma = pltpu.VMEM, pltpu.SemaphoreType.DMA
    LK = (LAYERS, CHUNKS)
    scratch = [
        V((4, WIDTH), BF), V((2, 4, WIDTH), BF), V((WIDTH,), BF), pltpu.SMEM((8,), jnp.int32), V((8, 16), jnp.int32),
        V((WIDTH, HID), BF), V((WIDTH, HID), BF), V((HID, WIDTH), BF), V((256, WIDTH), BF),
        V((128, WIDTH), BF),
        V((CHUNKS, 2, NQ, 8, 512), BF),
        V((2, CHUNKS, 2, NQ, 32, 128), BF),
        V((64, WIDTH), BF), V((128, WIDTH), BF),
        V((*LK, 8, 16, 1024), BF), V((*LK, 8, 16, 1024), BF),
        V((*LK, 8, 8, HID), BF), V((CHUNKS, 80, HID), BF),
        V((*LK, NQ, 32, 128), F32),
        V((*LK, NQ, 32, 128), BF), V((*LK, NQ, 32, 128), BF),
        V((CHUNKS, NQ, 32, 128), BF), V((CHUNKS, NQ, 32, 128), BF),
        V((NQ, 8, 128), BF), V((NQ, 8, 128), BF),
        V((NQ, 8, 128), F32), V((8, 8, 128), BF), V((8, 8, 128), BF),
        V((8, 8, 128), BF), V((NQ, 8, 8, 128), BF), V((NQ, 8, 128), BF),
        V((CHUNKS, 2, 4, 8, WIDTH), F32),
        V((CHUNKS, 32, 128), F32),
        V((2, CHUNKS, NQ, 8, 512), BF), V((CHUNKS, NQ, 8, 512), BF),
        V((CHUNKS, 8, 2, 8, 512), BF), V((CHUNKS, 8, 512), F32),
        V((CHUNKS, 8, 512), BF), V((CHUNKS, 8, 512), BF),
        dma((9,)), dma((48,)), dma((CHUNKS, NQ)), dma((CHUNKS,)), dma((NQ,)),
        dma((CHUNKS, NQ)), dma((CHUNKS,)), dma(LK), dma((*LK, 8)),
        dma((*LK, 2)), dma((CHUNKS,)), dma((1,)), dma((1,)), dma((1,)), dma((CHUNKS,)), dma((CHUNKS,)), dma((CHUNKS,)),
    ]
    both = pl.pallas_call(
        kernel,
        out_shape=jax.ShapeDtypeStruct((2, 4, WIDTH), BF),
        in_specs=[hbm] * 9,
        out_specs=vmem,
        scratch_shapes=scratch,
        compiler_params=pltpu.CompilerParams(
            collective_id=0, has_side_effects=True, vmem_limit_bytes=56 * 2**20
        ),
        name="beam_steps",
    )(
        beam_states, step_tokens, norm_gain, kept_beams, prompt_ids,
        w_gate, w_up, w_down, prompt_table,
    )
    return both[0], both[1]


def solution(mesh):
    return jax.shard_map(
        on_device,
        mesh=mesh,
        in_specs=(
            P("gy", "gx"),
            P(None, "gy", "gx"),
            P("gx"),
            P("gx", "gy"),
            P("gx", "gy"),
            P("gy", "gx"),
            P(None, "gx"),
            P(),
            P(),
        ),
        out_specs=(P("gy", "gx"), P("gy", "gx")),
        check_vma=False,
    )
```
